256 devices in a mesh: dp: 8 (over x, core), expert: 32 (over y, z).
Axes of the slice: x: 4, y: 4, z: 8, core: 2. Of those that a mesh axis runs over, the one named last changes fastest.
Arguments:
- cache_lat: bfloat16 [12288, 64, 512], P(('dp', 'expert')), may hold values from -6 to 6
- cache_rope: bfloat16 [12288, 4096], P(('dp', 'expert')), may hold values from -6 to 6
- page_scale: bfloat16 [12288], P(('dp', 'expert')), may hold values from 0.5 to 2
- move_list: int32 [256, 8, 4], P(('dp', 'expert')), may hold values from 0 to 47
- page_table: int32 [512, 32], P(('dp', 'expert')), may hold values from 0 to 79, as said below
- lengths: int32 [512], P(('dp', 'expert')), may hold values from 961 to 2048, as said below
- q_lat: bfloat16 [512, 2, 64, 512], P(('dp', 'expert')), may hold values from -72 to 72
- q_rope: bfloat16 [512, 2, 64, 64], P(('dp', 'expert')), may hold values from -12 to 12
- new_lat: bfloat16 [512, 2, 512], P(('dp', 'expert')), may hold values from -6 to 6
- new_rope: bfloat16 [512, 2, 64], P(('dp', 'expert')), may hold values from -6 to 6
- w_uv: bfloat16 [64, 512, 128], P('expert'), may hold values from -6 to 6
- w_out: bfloat16 [8192, 3584], P('expert'), may hold values from -0.0625 to 0.0625
- residual: bfloat16 [1024, 3584], P(('dp', 'expert')), may hold values from -400 to 400
- norm_gain: float32 [3584], replicated, may hold values from 0.1 to 1.9
- w_router: bfloat16 [3584, 32], replicated, may hold values from -0.09375 to 0.09375
- routes: int32 [1024, 8], P(('dp', 'expert')), may hold values from 0 to 31, all different within a row; in each aligned block of 4 rows (0 to 3, 4 to 7, ...) at most 2 rows name the same one
- w_gate: bfloat16 [32, 3584, 2048], P('expert', None, 'dp'), may hold values from -0.09375 to 0.09375
- w_up: bfloat16 [32, 3584, 2048], P('expert', None, 'dp'), may hold values from -0.09375 to 0.09375
- w_down: bfloat16 [32, 2048, 3584], P('expert', 'dp'), may hold values from -0.125 to 0.125
Outputs:
- attn_out: bfloat16 [1024, 3584], P(('dp', 'expert'))
- moe_out: bfloat16 [1024, 3584], P(('dp', 'expert'))
The draws below stay inside these ranges and needn't reach their ends.
Inputs may be any that keep to these rules, and one draw needn't show every extreme that they name: `lengths`: cached tokens of a rollout besides its 2 new ones; some rollout holds 2048. `page_table`: a rollout names no page index twice. `routes`: among the rows of one device no expert is named more than 2 times; some expert is named exactly 2 times.
All inputs are finite; a program needn't handle non-finite values.
Results may differ from the reference program's by a relative error of at most 0.03.
Values may be sent and summed in bfloat16 or wider, within the bound.
A program may use at most 128 MiB of HBM per device.

```python
import math
import jax
import jax.numpy as jnp
import numpy as np
from jax import lax

D = 3584
FF = 2048
LAT = 512
ROPE = 64
VDIM = 128
TOP = 8
NEXT = 2
PAGE = 64
R_DEV = 2
MAXP = 32
MOVES = 4
SLOTS = 48
HEADS = 64
EXPERTS = 32
CAP = 2
ROLLOUTS = 512
TOKENS = 1024
POOL = 12288
VIEW = 80
N_DP = 8
N_EXPERT = 32


def shared_latent(key):
    latent_base = jnp.clip(jax.random.normal(key, (ROLLOUTS, NEXT, LAT), jnp.float32), -6.0, 6.0)
    return latent_base


def shared_rope(key):
    return jnp.clip(jax.random.normal(jax.random.fold_in(key, 63), (ROLLOUTS, NEXT, ROPE), jnp.float32), -6.0, 6.0)


def table_and_lengths(key):
    keys = jax.random.split(jax.random.fold_in(key, 40), 6)
    moved_total = N_DP * MOVES
    index_ids = jnp.arange(VIEW, dtype=jnp.int32)
    position = jnp.arange(ROLLOUTS, dtype=jnp.int32) % R_DEV
    is_moved = index_ids >= SLOTS
    owned = ((index_ids - SLOTS) % R_DEV)[None, :] == position[:, None]
    priority = jnp.where(is_moved[None, :] & owned, 0, 1).astype(jnp.int32)
    noise = jax.random.randint(keys[0], (ROLLOUTS, VIEW), 0, 4096).astype(jnp.int32)
    score = (priority * 4096 + noise) * VIEW + index_ids[None, :]
    order = jnp.argsort(score, axis=-1, stable=True)[:, :MAXP].astype(jnp.int32)
    extra = (position < moved_total % R_DEV).astype(jnp.int32)
    owned_count = jnp.minimum(moved_total // R_DEV + extra, MAXP)
    floor_len = jnp.maximum(1, (owned_count - 1) * PAGE + 1)
    longest = MAXP * PAGE
    span = longest - floor_len + 1
    first_draw = jax.random.randint(keys[1], (ROLLOUTS,), 0, 1 << 20) % span
    second_draw = jax.random.randint(keys[2], (ROLLOUTS,), 0, 1 << 20) % span
    third_draw = jax.random.randint(keys[3], (ROLLOUTS,), 0, 1 << 20) % span
    short_len = floor_len + jnp.minimum(jnp.minimum(first_draw, second_draw), third_draw)
    tail_flag = jax.random.randint(keys[4], (ROLLOUTS,), 0, 16) == 0
    forced = jax.random.randint(keys[5], (), 0, ROLLOUTS)
    tail_flag = tail_flag | (jnp.arange(ROLLOUTS, dtype=jnp.int32) == forced)
    lengths_out = jnp.where(tail_flag, longest, short_len).astype(jnp.int32)
    return (order, lengths_out)


def draw_page_table(key, part):
    order, lengths_out = table_and_lengths(key)
    return order


def draw_lengths(key, part):
    order, lengths_out = table_and_lengths(key)
    return lengths_out


def draw_new_lat(key, part):
    latent_base = shared_latent(key)
    return latent_base.astype(jnp.bfloat16)


def draw_q_lat(key, part):
    key = jax.random.fold_in(key, 2)
    values = jnp.clip(jax.random.normal(key, (ROLLOUTS, NEXT, HEADS, LAT), jnp.float32), -6.0, 6.0)
    return values.astype(jnp.bfloat16)


def draw_q_rope(key, part):
    key = jax.random.fold_in(key, 6)
    values = jnp.clip(jax.random.normal(key, (ROLLOUTS, NEXT, HEADS, ROPE), jnp.float32), -6.0, 6.0)
    return values.astype(jnp.bfloat16)


def draw_new_rope(key, part):
    rope_base = shared_rope(key)
    values = rope_base
    return values.astype(jnp.bfloat16)


def draw_residual(key, part):
    key = jax.random.fold_in(key, 7)
    keys = jax.random.split(key, 3)
    row_scale = jnp.exp(jax.random.uniform(keys[0], (TOKENS, 1), jnp.float32) * 2.302585)
    column_scale = jnp.exp(jax.random.uniform(keys[1], (1, D), jnp.float32) * 2.302585)
    values = jnp.clip(jax.random.normal(keys[2], (TOKENS, D), jnp.float32), -4.0, 4.0)
    return (values * row_scale * column_scale).astype(jnp.bfloat16)


def plant(values, key, smallest, high):
    dims = values.shape
    index_at = [jax.random.randint(jax.random.fold_in(key, axis), (), 0, dims[axis]) for axis in range(len(dims))]
    values = values.at[tuple(index_at)].set(smallest)
    longest = dims.index(max(dims))
    index_at[longest] = (index_at[longest] + 1) % dims[longest]
    return values.at[tuple(index_at)].set(high)


def steps_of(key, dims, shards, smallest, largest):
    def one(dim, parts):
        steps = jax.random.uniform(jax.random.fold_in(jax.random.fold_in(key, 6), dim), (parts,), jnp.float32, smallest / len(shards), largest / len(shards))
        return jnp.repeat(jnp.exp(steps), dims[dim] // parts).reshape((-1,) + (1,) * (len(dims) - dim - 1))

    factor_of = one(*shards[0])
    for cut in shards[1:]:
        factor_of = factor_of * one(*cut)
    return factor_of


def deal_out(key, own, number, rows, count, top, reach, lean):
    sequence = jax.random.permutation(key, count)
    heavy_load, ordinary = portions_of(count, rows * top, reach, lean, True), portions_of(count, rows * top, reach, lean, False)
    places = jnp.arange(count)

    def named(tallies, offset_by):
        used = int((tallies > 0).sum())
        fixed = max(1, used // 4)
        moved = fixed + (places - fixed + offset_by * (used - fixed)) % max(1, count - fixed)
        return jnp.zeros((count,), jnp.int32).at[sequence[jnp.where(places < fixed, places, moved)]].set(jnp.asarray(tallies, jnp.int32))

    tallies = jnp.where(number % 4 == 0, named(heavy_load, number // 4), named(ordinary, number - number // 4 - 1))
    mixed = jax.random.permutation(jax.random.fold_in(own, 3), count)
    donor, receiver = mixed[0:count // 2 * 2:2], mixed[1:count // 2 * 2:2]
    slack = jnp.minimum(tallies[donor] - 1, reach - tallies[receiver]) // 2
    slack = jnp.where((donor == sequence[0]) | (receiver == sequence[0]) | (tallies[receiver] == 0), 0, jnp.maximum(slack, 0))
    moved = jax.random.randint(jax.random.fold_in(own, 4), (count // 2,), 0, 1 << 20) % (slack + 1)
    tallies = tallies.at[donor].add(-moved).at[receiver].add(moved)
    labels = jnp.searchsorted(jnp.cumsum(tallies), jnp.arange(rows * top), side="right").astype(jnp.int32)
    grid = labels.reshape(top, rows).T
    grid = grid[jax.random.permutation(jax.random.fold_in(own, 1), rows)]
    offset_by = jax.random.randint(jax.random.fold_in(own, 2), (rows, 1), 0, top)
    return jnp.take_along_axis(grid, (jnp.arange(top)[None, :] + offset_by) % top, axis=1)


def portions_of(number_of, total, limit, slope, full):
    portions = [(1 << 20) // math.isqrt(standing ** slope) + 1 for standing in range(1, number_of + 1)]
    largest = limit if full else min(limit, max(-(-total // number_of), total * portions[0] // sum(portions)))
    least = 1 if total - largest >= number_of - 1 else 0
    holding, spare = [largest] + [least] * (number_of - 1), total - largest - least * (number_of - 1)
    while spare > 0:
        free = [i for i in range(1, number_of) if holding[i] < largest] or [i for i in range(1, number_of) if holding[i] < limit]
        mass, left = sum([portions[i] for i in free]), spare
        for i in free:
            addition = min(limit - holding[i], max(1, left * portions[i] // mass), spare)
            holding[i] = holding[i] + addition
            spare = spare - addition
    return np.array(holding)


def centred(own_key, extent, spread, reach, shards=(), held_as=jnp.bfloat16):
    loudness = steps_of(own_key, extent, shards, -0.22, 0.18) if shards else 1.0
    array = jax.random.normal(own_key, extent, jnp.float32) * spread * loudness
    return jnp.minimum(jnp.maximum(array, -reach), reach).astype(held_as)


def setup_inputs(seed: int = 0) -> dict:
    streams_of = jax.random.split(jax.random.key(seed), 20)
    cache_lat = centred(streams_of[0], (POOL, PAGE, LAT), 1.0, 6.0, ((0, 256),))
    cache_rope = centred(streams_of[1], (POOL, PAGE * ROPE), 1.0, 6.0, ((0, 256),))
    page_scale = jnp.clip(jnp.exp(math.log(2.0) - 1.3862944 * jax.random.uniform(streams_of[2], (POOL,), jnp.float32) ** steps_of(streams_of[2], (POOL,), ((0, 256),), -0.2, 0.2)), 0.5, 2.0).astype(jnp.bfloat16)
    move_list = plant(jax.random.randint(streams_of[3], (N_DP * N_EXPERT, N_DP, MOVES), 0, SLOTS), jax.random.fold_in(streams_of[3], 1), 0, SLOTS - 1).astype(jnp.int32)
    page_table = draw_page_table(jax.random.fold_in(streams_of[19], 71), 0)
    lengths = draw_lengths(jax.random.fold_in(streams_of[19], 71), 0)
    q_lat = draw_q_lat(jax.random.fold_in(streams_of[19], 71), 0)
    q_rope = draw_q_rope(jax.random.fold_in(streams_of[19], 71), 0)
    new_lat = draw_new_lat(jax.random.fold_in(streams_of[19], 71), 0)
    new_rope = draw_new_rope(jax.random.fold_in(streams_of[19], 71), 0)
    w_uv = centred(streams_of[10], (HEADS, LAT, VDIM), 1.0, 6.0, ((0, 32),))
    w_out = centred(streams_of[11], (HEADS * VDIM, D), (HEADS * VDIM) ** -0.5, 0.0625, ((0, 32),))
    residual = draw_residual(jax.random.fold_in(streams_of[19], 71), 0)
    norm_gain = jnp.clip(1.0 + 0.18 * jax.random.normal(streams_of[13], (D,), jnp.float32), 0.1, 1.9)
    w_router = centred(streams_of[14], (D, EXPERTS), D ** -0.5, 0.09375)
    routes_keys = jax.random.split(jax.random.fold_in(streams_of[15], 1), TOKENS // (NEXT * R_DEV))
    routes_turns = jax.random.permutation(jax.random.fold_in(streams_of[15], 3), TOKENS // (NEXT * R_DEV))
    routes = jax.vmap(lambda own, number: deal_out(jax.random.fold_in(streams_of[15], 2), own, number, NEXT * R_DEV, EXPERTS, TOP, CAP, 2))(routes_keys, routes_turns).reshape((TOKENS, TOP))
    w_gate = centred(streams_of[16], (EXPERTS, D, FF), D ** -0.5, 0.09375, ((0, 32), (2, 8)))
    w_up = centred(streams_of[17], (EXPERTS, D, FF), D ** -0.5, 0.09375, ((0, 32), (2, 8)))
    w_down = centred(streams_of[18], (EXPERTS, FF, D), FF ** -0.5, 0.125, ((0, 32), (1, 8)))
    return {"cache_lat": cache_lat, "cache_rope": cache_rope, "page_scale": page_scale, "move_list": move_list, "page_table": page_table, "lengths": lengths, "q_lat": q_lat, "q_rope": q_rope, "new_lat": new_lat, "new_rope": new_rope, "w_uv": w_uv, "w_out": w_out, "residual": residual, "norm_gain": norm_gain, "w_router": w_router, "routes": routes, "w_gate": w_gate, "w_up": w_up, "w_down": w_down}


SCORE_SCALE = 0.07216878364870322
ROUTE_SCALE = 2.5
NORM_EPS = 1e-06

def pool_rows(move_list, page_table):
    owner = jnp.arange(ROLLOUTS, dtype=jnp.int32) // R_DEV
    row_group = owner // N_EXPERT
    column = owner % N_EXPERT
    shifted = jnp.maximum(page_table - SLOTS, 0).astype(jnp.int32)
    source = shifted // MOVES * N_EXPERT + column[:, None]
    picked = move_list[source, row_group[:, None], shifted % MOVES]
    remote = source * SLOTS + picked
    local = owner[:, None] * SLOTS + page_table
    return jnp.where(page_table < SLOTS, local, remote).astype(jnp.int32)

def reference(cache_lat, cache_rope, page_scale, move_list, page_table, lengths, q_lat, q_rope, new_lat, new_rope, w_uv, w_out, residual, norm_gain, w_router, routes, w_gate, w_up, w_down):
    page_rows = pool_rows(move_list, page_table)
    cached = MAXP * PAGE
    highest = lax.Precision.HIGHEST

    def attend(item):
        rows_here, length, query_lat, query_rope, fresh_lat, fresh_rope = item
        keys_lat = cache_lat[rows_here].astype(jnp.float32).reshape(cached, LAT)
        keys_rope = cache_rope[rows_here].astype(jnp.float32).reshape(cached, ROPE)
        token_scale = jnp.repeat(page_scale[rows_here].astype(jnp.float32), PAGE)
        qlf = query_lat.astype(jnp.float32)
        qrf = query_rope.astype(jnp.float32)
        old_scores = jnp.einsum('phl,tl->pht', qlf, keys_lat, precision=highest)
        old_scores = old_scores + jnp.einsum('phk,tk->pht', qrf, keys_rope, precision=highest)
        old_scores = old_scores * (token_scale * SCORE_SCALE)
        live = jnp.arange(cached, dtype=jnp.int32) < length
        old_scores = jnp.where(live[None, None, :], old_scores, -jnp.inf)
        fresh_lat_f = fresh_lat.astype(jnp.float32)
        new_scores = jnp.einsum('phl,ul->phu', qlf, fresh_lat_f, precision=highest)
        new_scores = new_scores + jnp.einsum('phk,uk->phu', qrf, fresh_rope.astype(jnp.float32), precision=highest)
        new_scores = new_scores * SCORE_SCALE
        causal = jnp.arange(NEXT)[None, :] <= jnp.arange(NEXT)[:, None]
        new_scores = jnp.where(causal[:, None, :], new_scores, -jnp.inf)
        peak = jnp.maximum(lax.optimization_barrier(jnp.max(old_scores, -1)), lax.optimization_barrier(jnp.max(new_scores, -1)))
        old_exp = jnp.exp(old_scores - peak[..., None])
        new_exp = jnp.exp(new_scores - peak[..., None])
        total = lax.optimization_barrier(jnp.sum(old_exp, -1)) + lax.optimization_barrier(jnp.sum(new_exp, -1))
        old_weights = (old_exp / total[..., None] * token_scale).astype(jnp.bfloat16)
        new_weights = (new_exp / total[..., None]).astype(jnp.bfloat16)
        result = jnp.einsum('pht,tl->phl', old_weights.astype(jnp.float32), keys_lat, precision=highest)
        result = result + jnp.einsum('phu,ul->phl', new_weights.astype(jnp.float32), fresh_lat_f, precision=highest)
        return result.astype(jnp.bfloat16)
    latent_out = lax.map(attend, (page_rows, lengths, q_lat, q_rope, new_lat, new_rope))
    head_values = jnp.einsum('rphl,hlv->rphv', latent_out.astype(jnp.float32), w_uv.astype(jnp.float32), precision=highest).astype(jnp.bfloat16)
    flat_values = head_values.reshape(TOKENS, HEADS * VDIM)
    attn_sum = jnp.dot(flat_values, w_out, preferred_element_type=jnp.float32)
    attn_out = attn_sum.astype(jnp.bfloat16)
    hidden = (residual.astype(jnp.float32) + attn_sum).astype(jnp.bfloat16)
    hidden_f = hidden.astype(jnp.float32)
    normed = (hidden_f * lax.rsqrt(lax.optimization_barrier(jnp.mean(hidden_f * hidden_f, -1, keepdims=True)) + NORM_EPS) * norm_gain).astype(jnp.bfloat16)
    logits = jnp.dot(normed, w_router, preferred_element_type=jnp.float32)
    onehot = routes[:, :, None] == jnp.arange(EXPERTS, dtype=jnp.int32)[None, None, :]
    selected = lax.optimization_barrier(jnp.sum(jnp.where(onehot, logits[:, None, :], jnp.float32(0.0)), -1))
    sig = jax.nn.sigmoid(selected)
    gates = ROUTE_SCALE * sig / lax.optimization_barrier(jnp.sum(sig, -1, keepdims=True))
    weight_table = lax.optimization_barrier(jnp.sum(jnp.where(onehot, gates[:, :, None], jnp.float32(0.0)), 1))

    def one_expert(carry, item):
        gate_w, up_w, down_w, column_weight = item
        gate_part = jnp.dot(normed, gate_w, preferred_element_type=jnp.float32)
        up_part = jnp.dot(normed, up_w, preferred_element_type=jnp.float32)
        expert_hidden = (jax.nn.silu(gate_part) * up_part).astype(jnp.bfloat16)
        expert_rows = jnp.dot(expert_hidden, down_w, preferred_element_type=jnp.float32)
        return (carry + column_weight[:, None] * expert_rows, None)
    start_sum = jnp.zeros((TOKENS, D), jnp.float32)
    moe_sum, _ = lax.scan(one_expert, start_sum, (w_gate, w_up, w_down, weight_table.T))
    return (attn_out, moe_sum.astype(jnp.bfloat16))
```

```python
import jax
import jax.numpy as jnp
from jax import lax
from jax.experimental import pallas as pl
from jax.experimental.pallas import tpu as pltpu
from jax.sharding import PartitionSpec as P

MESH = pl.DeviceIdType.MESH
SCORE_SCALE = 0.07216878364870322
ROUTE_SCALE = 2.5
NORM_EPS = 1e-06
NEG = -1e30
F32 = jnp.float32
BF16 = jnp.bfloat16
D = 3584
CH = 512
NK = 7
HALF = 1792


def dot(a, b):
    return lax.dot_general(a, b, (((1,), (0,)), ((), ())), preferred_element_type=F32)


def dot_nt(a, b):
    return lax.dot_general(a, b, (((1,), (1,)), ((), ())), preferred_element_type=F32)


def iota(shape, dim):
    return lax.broadcasted_iota(jnp.int32, shape, dim)


def kernel(
    mv_ref, ps_ref, lat_hbm, rope_ref, aux_ref, q_ref, qr_ref, nl_ref, nr_ref,
    wuv_hbm, wout_hbm, res_ref, gain_ref, wr_ref, rt_ref, wg_hbm, wu_hbm, wd_hbm,
    attn_ref, moe_ref,
    lat_v, wuv, wout, wg, wu, wd,
    slat, srope, rlat, rrope, newk, newr, q_l, q_r, m_s, l_s, o_s,
    so, ro, hv_s, pf, ps1, pr1, s_f, d_f, sp2, pr2, al_f, res_l, gain_l,
    q_s, qt_s, sd, rd, t_f, xr, pp, sr, ss, hb, hr, fb, fr, sret, rret,
    lsem, pg_s, pg_r, o_ss, o_rs, p1_s, p1_r, p2_s, p2_r, d_ss, d_rs, ag_s, ag_r, rs_s, rs_r, b_ss, b_rs,
):
    i = lax.axis_index("dp")
    j = lax.axis_index("expert")
    x, c, y, z = i // 2, i % 2, j // 8, j % 8

    def dp_to(dx, dc):
        return (((x + dx) % 4) * 2 + (c + dc) % 2, j)

    def ex_at(dy, dz):
        return ((y + dy + 4) % 4) * 8 + (z + dz + 8) % 8

    def rcopy(src, dst, send, recv, dev):
        return pltpu.make_async_remote_copy(
            src_ref=src, dst_ref=dst, send_sem=send, recv_sem=recv, device_id=dev, device_id_type=MESH
        )

    right, left, sib = dp_to(1, 0), dp_to(3, 0), dp_to(0, 1)

    loads = [
        pltpu.make_async_copy(a, b, lsem.at[n])
        for n, (a, b) in enumerate(
            [(lat_hbm, lat_v), (wuv_hbm, wuv), (wout_hbm, wout), (wg_hbm.at[0], wg), (wu_hbm.at[0], wu), (wd_hbm.at[0], wd)]
        )
    ]
    for cp in loads:
        cp.start()
    barrier = pltpu.get_barrier_semaphore()

    @pl.loop(1, 8)
    def _(k):
        pl.semaphore_signal(barrier, inc=1, device_id=dp_to(k // 2, k % 2), device_id_type=MESH)

    @pl.loop(1, 32)
    def _(k):
        pl.semaphore_signal(barrier, inc=1, device_id=(i, ex_at(k // 8, k % 8)), device_id_type=MESH)

    loads[0].wait()

    low_lane = iota((64, 128), 1) < 64
    low16 = iota((16, 128), 1) < 64
    row16 = iota((16, 128), 0)

    @pl.loop(0, 8)
    def _(k):
        dest = ((x + k // 2) % 4) * 2 + (c + k % 2) % 2
        pages = [mv_ref[dest, m] for m in range(4)]
        for m in range(4):
            slat[k, m * 64 : (m + 1) * 64, :] = lat_v[pages[m]]
        for m in range(2):
            a = rope_ref[pages[2 * m]].astype(F32)
            b = rope_ref[pages[2 * m + 1]].astype(F32)
            srope[k, m * 64 : (m + 1) * 64, :] = jnp.where(low_lane, a, b).astype(BF16)
        scales = [ps_ref[pages[m]] for m in range(4)]
        first = jnp.where(low16, scales[0], scales[1])
        second = jnp.where(low16, scales[2], scales[3])
        srope[k, 128:144, :] = jnp.where(row16 == 0, first, second).astype(BF16)

    def page_copies(k):
        dev = dp_to(k // 2, k % 2)
        return (
            rcopy(slat.at[k], rlat.at[k], pg_s.at[0, k], pg_r.at[0, k], dev),
            rcopy(srope.at[k], rrope.at[k], pg_s.at[1, k], pg_r.at[1, k], dev),
        )

    pl.semaphore_wait(barrier, 38)

    @pl.loop(1, 8)
    def _(k):
        for cp in page_copies(k):
            cp.start()

    e32 = iota((32, 32), 1)
    sel = jnp.zeros((32, 32), F32)
    for kk in range(8):
        sel = jnp.where(rt_ref[:, kk : kk + 1] == e32, 1.0, sel)
    r32 = iota((32, 32), 0)
    earlier = jnp.where((r32 // 4 == e32 // 4) & (e32 % 4 < r32 % 4), 1.0, 0.0).astype(BF16)
    cum = dot(earlier, sel.astype(BF16))
    code = sel * (cum + 1.0)
    lane512 = iota((32, 512), 1)
    row512 = iota((32, 512), 0)
    spread = jnp.where(lane512 // 16 == row512, 1.0, 0.0).astype(BF16)
    codes = dot(code.astype(BF16), spread)
    want = ((lane512 // 8) % 2 + 1).astype(F32)
    qt = jnp.where((codes == want) & (row512 // 4 == lane512 % 8), 1.0, 0.0)
    qt_s[...] = qt
    q_s[...] = qt.T.astype(BF16)
    res_l[...] = jnp.zeros_like(res_l)
    gain_l[...] = jnp.zeros_like(gain_l)
    d_f[...] = jnp.zeros_like(d_f)
    for k in range(NK):
        res_l[4 * k : 4 * k + 4, :] = res_ref[:, k * CH : (k + 1) * CH].astype(F32)
        gain_l[4 * k : 4 * k + 4, :] = jnp.broadcast_to(gain_ref[:, k * CH : (k + 1) * CH], (4, CH))

    zeros64 = jnp.zeros((256, 64), F32)
    qr = qr_ref[...].astype(F32)
    q_l[...] = jnp.concatenate([qr, zeros64], axis=1).astype(BF16)
    q_r[...] = jnp.concatenate([zeros64, qr], axis=1).astype(BF16)
    newk[...] = jnp.zeros_like(newk)
    newr[...] = jnp.zeros_like(newr)
    newk[0:4, :] = nl_ref[...].astype(F32)
    newr[0:4, 0:64] = nr_ref[...].astype(F32)
    nk = newk[...].astype(BF16)
    s = (dot_nt(q_ref[...], nk) + dot_nt(q_l[...], newr[...].astype(BF16))) * SCORE_SCALE
    row = iota((256, 128), 0)
    col = iota((256, 128), 1)
    ok = (col < 4) & (col // 2 == row // 128) & (col % 2 <= (row // 64) % 2)
    s = jnp.where(ok, s, NEG)
    m = jnp.max(s, -1, keepdims=True)
    p = jnp.exp(s - m)
    m_s[...] = jnp.broadcast_to(m, (256, 128))
    l_s[...] = jnp.broadcast_to(jnp.sum(p, -1, keepdims=True), (256, 128))
    o_s[...] = dot(p.astype(BF16), nk)

    def attend(keys, s_rope, scale, bias0, bias1):
        s = (dot_nt(q_ref[...], keys) + s_rope) * (scale * SCORE_SCALE)
        s = jnp.concatenate([s[:128] + bias0, s[128:] + bias1], axis=0)
        m_old = m_s[:, 0:1]
        m_new = jnp.maximum(m_old, jnp.max(s, -1, keepdims=True))
        p = jnp.exp(s - m_new)
        alpha = jnp.exp(m_old - m_new)
        m_s[...] = jnp.broadcast_to(m_new, (256, 128))
        l_s[...] = jnp.broadcast_to(l_s[:, 0:1] * alpha + jnp.sum(p, -1, keepdims=True), (256, 128))
        o_s[...] = o_s[...] * alpha + dot((p * scale).astype(BF16), keys)

    @pl.loop(0, 12)
    def _(n):
        keys = lat_v[pl.ds(n * 4, 4)].reshape(256, 512)
        ropes = rope_ref[pl.ds(n * 4, 4)].reshape(256, 128)
        a = aux_ref[n]
        attend(keys, dot_nt(q_l[...], ropes), a[0:1], a[1:2], a[2:3])

    def attend_moved(k, lat_at, rope_at):
        source = ((x - k // 2 + 4) % 4) * 2 + (c + k % 2) % 2
        a = aux_ref[12 + source]
        ropes = rope_at[0:128, :]
        lo = dot_nt(q_l[...], ropes)
        hi = dot_nt(q_r[...], ropes)
        s_rope = jnp.concatenate([lo[:, :64], hi[:, :64], lo[:, 64:], hi[:, 64:]], axis=1)
        sc = rope_at[128:144, :].astype(F32)
        scale = jnp.concatenate([sc[0:1], sc[1:2]], axis=1)
        attend(lat_at[...], s_rope, scale, a[1:2], a[2:3])

    attend_moved(0, slat.at[0], srope.at[0])

    @pl.loop(1, 8)
    def _(k):
        for cp in page_copies(k):
            cp.wait_recv()
        attend_moved(k, rlat.at[k], rrope.at[k])

    loads[1].wait()
    loads[2].wait()

    o = (o_s[...] / l_s[:, 0:1]).astype(BF16)
    pr = iota((256, 256), 0)
    pc = iota((256, 256), 1)
    perm = jnp.where(pc == (pr // 2 % 4) * 64 + (pr // 8) * 2 + pr % 2, 1.0, 0.0).astype(BF16)
    oa = dot(perm, o[:, :256]).reshape(32, 8, 256)
    ob = dot(perm, o[:, 256:]).reshape(32, 8, 256)
    so[...] = jnp.concatenate([oa, ob], axis=1).astype(BF16)

    def o_copy(k):
        e = ex_at(k // 8, k % 8)
        return rcopy(so.at[e], ro.at[j], o_ss.at[k], o_rs.at[k], (i, e))

    @pl.loop(1, 32)
    def _(k):
        o_copy(k).start()

    ro[j] = so[j]

    @pl.loop(1, 32)
    def _(k):
        o_copy(k).wait_recv()

    got = ro[...].astype(F32)
    g0 = got[:, :8, :].reshape(256, 256).astype(BF16)
    g1 = got[:, 8:, :].reshape(256, 256).astype(BF16)
    wcat = jnp.concatenate([wuv[0], wuv[1]], axis=1)
    hv = dot(g0, wcat[:256]) + dot(g1, wcat[256:])
    hv = jnp.where(pr % 2 == pc // 128, hv, 0.0).astype(BF16)
    fold = jnp.where(iota((128, 256), 0) == iota((128, 256), 1) // 2, 1.0, 0.0).astype(BF16)
    hv_s[...] = dot(fold, hv).astype(BF16)

    for k in range(NK):
        w = slice(k * CH, (k + 1) * CH)
        part = dot(hv_s[...], wout[:, w]).reshape(4, 32, CH)
        pf[:, :, w] = part
        ps1[:, :, w] = part.astype(BF16)

    def y_copy(n):
        yy = (y + n) % 4
        return rcopy(ps1.at[yy], pr1.at[n], p1_s.at[n], p1_r.at[n], (i, ex_at(n, 0)))

    for n in (1, 3, 2):
        y_copy(n).start()
    for n in (1, 3, 2):
        y_copy(n).wait_recv()
    s_f[...] = pf[y] + pr1[1].astype(F32) + pr1[2].astype(F32) + pr1[3].astype(F32)
    for zz in range(8):
        for k in range(NK):
            d_f[zz, 4 * k : 4 * k + 4, :] = s_f[4 * zz : 4 * zz + 4, k * CH : (k + 1) * CH]
    sp2[...] = d_f[...].astype(BF16)

    def z_copy(n):
        zz = (z + n) % 8
        return rcopy(sp2.at[zz], pr2.at[n], p2_s.at[n], p2_r.at[n], (i, ex_at(0, n)))

    for n in (4, 3, 5, 2, 6, 1, 7):
        z_copy(n).start()
    total = d_f[z]
    for n in range(1, 8):
        z_copy(n).wait_recv()
        total = total + pr2[n].astype(F32)
    al_f[...] = total

    hidden = (res_l[...] + total).astype(BF16).astype(F32)
    same = jnp.where(r32 % 4 == e32 % 4, 1.0, 0.0)
    sq = jnp.broadcast_to(jnp.sum(hidden * hidden, -1, keepdims=True), (32, 128))
    sq = jnp.dot(same, sq, precision=lax.Precision.HIGHEST, preferred_element_type=F32)
    normed = (hidden * lax.rsqrt(sq[:, 0:1] / D + NORM_EPS) * gain_l[...]).astype(BF16)
    sd[...] = dot(q_s[...], normed).astype(BF16).reshape(32, 16, CH)

    def d_copy(k):
        e = ex_at(k // 8, k % 8)
        return rcopy(sd.at[e], rd.at[k], d_ss.at[k], d_rs.at[k], (i, e))

    @pl.loop(1, 32)
    def _(k):
        d_copy(k).start()

    rd[0] = sd[j]

    acc = jnp.zeros((32, 32), F32)
    for k in range(NK):
        lg = dot_nt(normed, wr_ref[:, k * CH : (k + 1) * CH])
        acc = acc + jnp.where(r32 // 4 == k, lg, 0.0)
    logits = jnp.dot(same, acc, precision=lax.Precision.HIGHEST, preferred_element_type=F32)
    sig = sel / (1.0 + jnp.exp(-logits))
    gates = ROUTE_SCALE * sig / jnp.sum(sig, -1, keepdims=True)
    g_hi = gates.astype(BF16)
    g_lo = (gates - g_hi.astype(F32)).astype(BF16)
    c_hi = (dot(g_hi, spread) * qt_s[...]).astype(BF16)
    c_lo = (dot(g_lo, spread) * qt_s[...]).astype(BF16)
    for k in range(NK):
        attn_ref[:, k * CH : (k + 1) * CH] = al_f[4 * k : 4 * k + 4, :].astype(BF16)
    for n in range(3, 6):
        loads[n].wait()

    def ag(g, n):
        lo, hi = pl.ds(0, HALF), pl.ds(HALF, HALF)
        src, dst, dev = [
            (xr.at[g, 0], xr.at[g, 3], right),
            (xr.at[g, 0], xr.at[g, 1], left),
            (xr.at[g, 3, :, lo], xr.at[g, 2, :, lo], right),
            (xr.at[g, 1, :, hi], xr.at[g, 2, :, hi], left),
            (xr.at[g, 0], xr.at[g, 4], sib),
            (xr.at[g, 3], xr.at[g, 7], sib),
            (xr.at[g, 1], xr.at[g, 5], sib),
            (xr.at[g, 2], xr.at[g, 6], sib),
        ][n]
        return rcopy(src, dst, ag_s.at[g, n], ag_r.at[g, n], dev)

    def rs(g, n):
        lo, hi = pl.ds(0, HALF), pl.ds(HALF, HALF)
        src, dst, dev = [
            (pp.at[g, pl.ds(4, 4)], sr.at[g], sib),
            (hb.at[g, :, lo], hr.at[g, 0], right),
            (hb.at[g, :, hi], hr.at[g, 1], left),
            (fb.at[g, 0], fr.at[g, 0], right),
            (fb.at[g, 1], fr.at[g, 1], left),
        ][n]
        return rcopy(src, dst, rs_s.at[g, n], rs_r.at[g, n], dev)

    def b_copy(k):
        e = ex_at(-(k // 8), -(k % 8))
        return rcopy(sret.at[k], rret.at[j], b_ss.at[k], b_rs.at[k], (i, e))

    def stage_a(g):
        @pl.loop(0, 8)
        def _(n):
            @pl.when(g * 8 + n > 0)
            def _():
                d_copy(g * 8 + n).wait_recv()

        got = rd[pl.ds(g * 8, 8)].reshape(128, CH).astype(F32)
        for b in range(4):
            t_f[b * 128 : (b + 1) * 128, :] = got[:, b * 128 : (b + 1) * 128]
        for k in range(NK):
            for b in range(4):
                at = k * CH + b * 128
                xr[g, 0, :, at : at + 128] = t_f[pl.ds(b * 128 + k, 16, stride=8), :].astype(BF16)
        for n in (0, 1, 4):
            ag(g, n).start()

    def stage_b(g):
        ag(g, 0).wait_recv()
        ag(g, 2).start()
        ag(g, 5).start()
        ag(g, 1).wait_recv()
        ag(g, 3).start()
        ag(g, 6).start()

    def stage_c(g):
        ag(g, 2).wait_recv()
        ag(g, 3).wait_recv()
        ag(g, 7).start()
        for n in range(4, 8):
            ag(g, n).wait_recv()

    def stage_d(g):
        rows = xr[g].reshape(128, D)
        gate = dot(rows, wg[...])
        up = dot(rows, wu[...])
        h = (gate / (1.0 + jnp.exp(-gate)) * up).astype(BF16)
        for k in range(NK):
            w = slice(k * CH, (k + 1) * CH)
            pp[g, :, :, w] = dot(h, wd[:, w]).astype(BF16).reshape(8, 16, CH)
        rs(g, 0).start()

    def stage_e(g):
        rs(g, 0).wait_recv()
        ss[g] = pp[g, 0:4].astype(F32) + sr[g].astype(F32)
        hb[g] = ss[g, 2].astype(BF16)
        rs(g, 1).start()
        rs(g, 2).start()

    def stage_f(g):
        rs(g, 1).wait_recv()
        fb[g, 0, :, 0:HALF] = (ss[g, 1, :, 0:HALF] + hr[g, 0].astype(F32)).astype(BF16)
        fb[g, 0, :, HALF:] = ss[g, 1, :, HALF:].astype(BF16)
        rs(g, 3).start()
        rs(g, 2).wait_recv()
        fb[g, 1, :, 0:HALF] = ss[g, 3, :, 0:HALF].astype(BF16)
        fb[g, 1, :, HALF:] = (ss[g, 3, :, HALF:] + hr[g, 1].astype(F32)).astype(BF16)
        rs(g, 4).start()

    def stage_g(g):
        rs(g, 3).wait_recv()
        rs(g, 4).wait_recv()
        for b in range(4):
            for k in range(NK):
                w = slice(k * CH + b * 128, k * CH + b * 128 + 128)
                v = ss[g, 0, :, w] + fr[g, 0, :, w].astype(F32) + fr[g, 1, :, w].astype(F32)
                t_f[pl.ds(b * 128 + k, 16, stride=8), :] = v
            t_f[pl.ds(b * 128 + 7, 16, stride=8), :] = jnp.zeros((16, 128), F32)
        back = jnp.concatenate([t_f[b * 128 : (b + 1) * 128, :] for b in range(4)], axis=1)
        sret[pl.ds(g * 8, 8)] = back.astype(BF16).reshape(8, 16, CH)

        @pl.loop(0, 8)
        def _(n):
            @pl.when(g * 8 + n > 0)
            def _():
                b_copy(g * 8 + n).start()

    stages = [(stage_a, 0), (stage_b, 1), (stage_c, 2), (stage_d, 2), (stage_e, 3), (stage_f, 4), (stage_g, 5)]

    @pl.loop(0, 9)
    def _(t):
        for fn, lag in stages:

            @pl.when((t >= lag) & (t < lag + 4))
            def _(fn=fn, lag=lag):
                fn(t - lag)

    rret[j] = sret[0]

    @pl.loop(1, 32)
    def _(k):
        b_copy(k).wait_recv()

    rows = rret[...].reshape(512, CH)
    al_f[...] = dot(c_hi, rows) + dot(c_lo, rows)
    for k in range(NK):
        moe_ref[:, k * CH : (k + 1) * CH] = al_f[4 * k : 4 * k + 4, :].astype(BF16)

    @pl.loop(1, 8)
    def _(k):
        for cp in page_copies(k):
            cp.wait_send()

    @pl.loop(1, 32)
    def _(k):
        o_copy(k).wait_send()
        d_copy(k).wait_send()
        b_copy(k).wait_send()

    for n in (1, 2, 3):
        y_copy(n).wait_send()
    for n in range(1, 8):
        z_copy(n).wait_send()

    @pl.loop(0, 4)
    def _(g):
        for n in range(8):
            ag(g, n).wait_send()
        for n in range(5):
            rs(g, n).wait_send()


def body(
    cache_lat, cache_rope, page_scale, move_list, page_table, lengths, q_lat, q_rope, new_lat, new_rope,
    w_uv, w_out, residual, norm_gain, w_router, routes, w_gate, w_up, w_down,
):
    slots, page = cache_lat.shape[0], cache_lat.shape[1]
    rope3 = cache_rope.reshape(slots, page, 64)
    rope2 = jnp.concatenate([rope3, rope3], axis=-1)
    ps = page_scale.astype(F32)
    names = page_table[:, :, None] == jnp.arange(80, dtype=jnp.int32)
    left_tokens = lengths[:, None] - jnp.arange(32, dtype=jnp.int32)[None, :] * page
    limit = jnp.max(jnp.where(names, left_tokens[:, :, None], 0), axis=1)
    bias = jnp.where(jnp.arange(page, dtype=jnp.int32) < limit[:, :, None], 0.0, NEG).reshape(2, 20, 256)
    token_scale = jnp.broadcast_to(jnp.pad(ps, (0, 32))[:, None], (80, page)).reshape(1, 20, 256)
    aux = jnp.concatenate([token_scale, bias, jnp.zeros((5, 20, 256), F32)], axis=0).transpose(1, 0, 2)
    routes32 = jnp.tile(routes, (8, 1))

    any_spec = pl.BlockSpec(memory_space=pl.ANY)
    vmem = pl.BlockSpec(memory_space=pltpu.VMEM)
    smem = pl.BlockSpec(memory_space=pltpu.SMEM)
    dma = pltpu.SemaphoreType.DMA
    vm = pltpu.VMEM
    attn, moe = pl.pallas_call(
        kernel,
        out_shape=[jax.ShapeDtypeStruct((4, D), BF16)] * 2,
        in_specs=[smem, smem, any_spec] + [vmem] * 6 + [any_spec] * 2 + [vmem] * 4 + [any_spec] * 3,
        out_specs=[vmem] * 2,
        scratch_shapes=[
            vm((48, 64, 512), BF16), vm((2, 512, 128), BF16), vm((256, D), BF16),
            vm((D, 256), BF16), vm((D, 256), BF16), vm((256, D), BF16),
            vm((8, 256, 512), BF16), vm((8, 144, 128), BF16), vm((8, 256, 512), BF16), vm((8, 144, 128), BF16),
            vm((128, 512), F32), vm((128, 128), F32), vm((256, 128), BF16), vm((256, 128), BF16),
            vm((256, 128), F32), vm((256, 128), F32), vm((256, 512), F32),
            vm((32, 16, 256), BF16), vm((32, 16, 256), BF16), vm((128, 256), BF16),
            vm((4, 32, D), F32), vm((4, 32, D), BF16), vm((4, 32, D), BF16), vm((32, D), F32),
            vm((8, 32, CH), F32), vm((8, 32, CH), BF16), vm((8, 32, CH), BF16),
            vm((32, CH), F32), vm((32, CH), F32), vm((32, CH), F32),
            vm((512, 32), BF16), vm((32, 512), F32), vm((32, 16, CH), BF16), vm((32, 16, CH), BF16),
            vm((512, 128), F32), vm((4, 8, 16, D), BF16), vm((4, 8, 16, D), BF16), vm((4, 4, 16, D), BF16),
            vm((4, 4, 16, D), F32), vm((4, 16, D), BF16), vm((4, 2, 16, HALF), BF16),
            vm((4, 2, 16, D), BF16), vm((4, 2, 16, D), BF16), vm((32, 16, CH), BF16), vm((32, 16, CH), BF16),
            dma((6,)), dma((2, 8)), dma((2, 8)), dma((32,)), dma((32,)), dma((4,)), dma((4,)),
            dma((8,)), dma((8,)), dma((32,)), dma((32,)), dma((4, 8)), dma((4, 8)), dma((4, 5)), dma((4, 5)),
            dma((32,)), dma((32,)),
        ],
        compiler_params=pltpu.CompilerParams(
            collective_id=0, has_side_effects=True, vmem_limit_bytes=60 * 2**20
        ),
        name="step",
    )(
        move_list[0], ps, cache_lat, rope2, aux, q_lat.reshape(256, 512), q_rope.reshape(256, 64),
        new_lat.reshape(4, 512), new_rope.reshape(4, 64), w_uv, w_out, residual, norm_gain.reshape(1, D),
        w_router.T, routes32, w_gate, w_up, w_down,
    )
    return attn, moe


def solution(mesh):
    both = ("dp", "expert")
    return jax.shard_map(
        body,
        mesh=mesh,
        in_specs=(
            P(both, None, None), P(both, None), P(both), P(both, None, None), P(both, None), P(both),
            P(both, None, None, None), P(both, None, None, None), P(both, None, None), P(both, None, None),
            P("expert", None, None), P("expert", None), P(both, None), P(), P(), P(both, None),
            P("expert", None, "dp"), P("expert", None, "dp"), P("expert", "dp", None),
        ),
        out_specs=(P(both, None), P(both, None)),
        check_vma=False,
    )
```

```python
import jax
import jax.numpy as jnp
from jax import lax
from jax.experimental import pallas as pl
from jax.experimental.pallas import tpu as pltpu
from jax.sharding import PartitionSpec as P

MESH = pl.DeviceIdType.MESH
SCORE_SCALE = 0.07216878364870322
ROUTE_SCALE = 2.5
NORM_EPS = 1e-06
NEG = -1e30
F32 = jnp.float32
BF16 = jnp.bfloat16
D = 3584
CH = 512
NK = 7
HALF = 1792


def dot(a, b):
    return lax.dot_general(a, b, (((1,), (0,)), ((), ())), preferred_element_type=F32)


def dot_nt(a, b):
    return lax.dot_general(a, b, (((1,), (1,)), ((), ())), preferred_element_type=F32)


def iota(shape, dim):
    return lax.broadcasted_iota(jnp.int32, shape, dim)


def kernel(
    mv_hbm, ps_hbm, len_hbm, pt_hbm, lat_hbm, rope_hbm, q_hbm, qr_hbm, nl_hbm, nr_hbm,
    wuv_hbm, wout_hbm, res_hbm, gain_hbm, wr_hbm, rt_hbm, wg_hbm, wu_hbm, wd_hbm,
    out_ref,
    mv_ref, ps_ref, len_ref, pt_ref, rope_raw, q_ref, qr_ref, nl_ref, nr_ref, res_ref, gain_ref, wr_ref, rt_ref,
    rope_f, rope_ref, bias_s, scale_s, rt_s,
    lat_v, wuv, wout, wg, wu, wd,
    slat, srope, rlat, rrope, newk, newr, q_l, q_r, m_s, l_s, o_s,
    so, ro, s_f, d_f, sp2, pr2, al_f, res_l, gain_l,
    q_s, qt_s, sd, rd, t_f, xr, pp, sr, ss, hb, hr, fb, fr, sret, rret,
    lsem, pg_s, pg_r, w_ss, w_rs, o_ss, o_rs, p2_s, p2_r, d_ss, d_rs, ag_s, ag_r, rs_s, rs_r, b_ss, b_rs,
):
    i = lax.axis_index("dp")
    j = lax.axis_index("expert")
    x, c, y, z = i // 2, i % 2, j // 8, j % 8

    def dp_to(dx, dc):
        return (((x + dx) % 4) * 2 + (c + dc) % 2, j)

    def ex_at(dy, dz):
        return ((y + dy + 4) % 4) * 8 + (z + dz + 8) % 8

    def rcopy(src, dst, send, recv, dev):
        return pltpu.make_async_remote_copy(
            src_ref=src, dst_ref=dst, send_sem=send, recv_sem=recv, device_id=dev, device_id_type=MESH
        )

    right, left, sib = dp_to(1, 0), dp_to(3, 0), dp_to(0, 1)
    barrier = pltpu.get_barrier_semaphore()

    @pl.loop(1, 8)
    def _(k):
        pl.semaphore_signal(barrier, inc=1, device_id=dp_to(k // 2, k % 2), device_id_type=MESH)

    pairs = [
        (mv_hbm.at[0], mv_ref), (ps_hbm, ps_ref), (lat_hbm, lat_v), (rope_hbm, rope_raw), (wuv_hbm, wuv.at[0]),
        (wout_hbm, wout.at[0]), (len_hbm, len_ref), (pt_hbm, pt_ref), (q_hbm, q_ref), (qr_hbm, qr_ref),
        (nl_hbm, nl_ref), (nr_hbm, nr_ref), (rt_hbm, rt_ref), (res_hbm, res_ref), (gain_hbm, gain_ref),
        (wr_hbm, wr_ref), (wg_hbm.at[0], wg), (wu_hbm.at[0], wu), (wd_hbm.at[0], wd),
    ]
    loads = [pltpu.make_async_copy(a, b, lsem.at[n]) for n, (a, b) in enumerate(pairs)]
    for cp in loads:
        cp.start()

    @pl.loop(1, 32)
    def _(k):
        pl.semaphore_signal(barrier, inc=1, device_id=(i, ex_at(k // 8, k % 8)), device_id_type=MESH)

    for n in range(3):
        loads[n].wait()

    def dest_of(k):
        return ((x + k // 2) % 4) * 2 + (c + k % 2) % 2

    @pl.loop(0, 8)
    def _(k):
        dest = dest_of(k)
        for m in range(4):
            slat[k, m * 64 : (m + 1) * 64, :] = lat_v[mv_ref[m, dest]]

    def page_copy(k, n):
        dev = dp_to(k // 2, k % 2)
        if n == 0:
            return rcopy(slat.at[k], rlat.at[k], pg_s.at[0, k], pg_r.at[0, k], dev)
        return rcopy(srope.at[k], rrope.at[k], pg_s.at[1, k], pg_r.at[1, k], dev)

    up_y, down_y = (i, ex_at(1, 0)), (i, ex_at(-1, 0))

    def w_copy(kind, n):
        if kind == 0:
            own = [wuv.at[d, c] for d in range(4)]
            up = [wuv.at[d, c, pl.ds(0, 256)] for d in range(4)]
            down = [wuv.at[d, c, pl.ds(256, 256)] for d in range(4)]
            near_up = near_down = own
        else:
            rows = pl.ds(c * 128, 128)
            own = [wout.at[d, rows] for d in range(4)]
            up = [wout.at[d, rows, pl.ds(0, HALF)] for d in range(4)]
            down = [wout.at[d, rows, pl.ds(HALF, HALF)] for d in range(4)]
            near_up, near_down = (up, down) if kind == 1 else (down, up)
        src, dst, dev = [
            (near_up[0], near_up[3], up_y),
            (near_down[0], near_down[1], down_y),
            (up[3], up[2], up_y),
            (down[1], down[2], down_y),
            (near_up[3], near_up[3], sib),
            (near_down[1], near_down[1], sib),
            (own[2], own[2], sib),
        ][n]
        return rcopy(src, dst, w_ss.at[kind, n], w_rs.at[kind, n], dev)

    pl.semaphore_wait(barrier, 38)

    @pl.loop(1, 8)
    def _(k):
        page_copy(k, 0).start()

    loads[4].wait()
    loads[5].wait()
    for kind in range(3):
        w_copy(kind, 0).start()
        w_copy(kind, 1).start()

    loads[3].wait()
    low48 = iota((48, 128), 1) < 64
    for g in range(32):
        v = rope_raw[:, g * 128 : (g + 1) * 128].astype(F32)
        w = pltpu.roll(v, 64, axis=1)
        rope_f[pl.ds(2 * g, 48, stride=64), :] = jnp.where(low48, v, w)
        rope_f[pl.ds(2 * g + 1, 48, stride=64), :] = jnp.where(low48, w, v)

    @pl.loop(0, 48)
    def _(n):
        rope_ref[n] = rope_f[pl.ds(pl.multiple_of(n * 64, 64), 64), :].astype(BF16)

    scales = jnp.concatenate([ps_ref[...].astype(F32).reshape(1, 48), jnp.zeros((1, 80), F32)], axis=1)
    scale_s[...] = jnp.broadcast_to(scales, (128, 128)).T

    def scale_of(v):
        return scale_s[pl.ds(v, 1), :]

    low_lane = iota((64, 128), 1) < 64
    low16 = iota((16, 128), 1) < 64
    row16 = iota((16, 128), 0)

    @pl.loop(0, 8)
    def _(k):
        dest = dest_of(k)
        pages = [mv_ref[m, dest] for m in range(4)]
        for m in range(2):
            a = rope_ref[pages[2 * m]].astype(F32)
            b = rope_ref[pages[2 * m + 1]].astype(F32)
            srope[k, m * 64 : (m + 1) * 64, :] = jnp.where(low_lane, a, b).astype(BF16)
        scales = [scale_of(pages[m]) for m in range(4)]
        first = jnp.where(low16, scales[0], scales[1])
        second = jnp.where(low16, scales[2], scales[3])
        srope[k, 128:144, :] = jnp.where(row16 == 0, first, second).astype(BF16)

    @pl.loop(1, 8)
    def _(k):
        page_copy(k, 1).start()

    for n in range(6, 16):
        loads[n].wait()
    page_id = iota((80, 32), 0)
    entry = iota((80, 32), 1)
    in_page = iota((80, 128), 1) % 64
    for r in range(2):
        fits = jnp.where(pt_ref[r : r + 1, :] == page_id, len_ref[r] - entry * 64, 0)
        limit = jnp.max(fits, axis=1, keepdims=True)
        bias_s[r] = jnp.where(in_page < limit, 0.0, NEG)
    low1 = iota((1, 128), 1) < 64

    def bias_of(r, v):
        b = [bias_s[r, pl.ds(v + m, 1), :] for m in range(4)]
        return jnp.concatenate([jnp.where(low1, b[0], b[1]), jnp.where(low1, b[2], b[3])], axis=1)

    for k in range(8):
        rt_s[4 * k : 4 * k + 4, :] = rt_ref[...]
    e32 = iota((32, 32), 1)
    sel = jnp.zeros((32, 32), F32)
    for kk in range(8):
        sel = jnp.where(rt_s[:, kk : kk + 1] == e32, 1.0, sel)
    r32 = iota((32, 32), 0)
    earlier = jnp.where((r32 // 4 == e32 // 4) & (e32 % 4 < r32 % 4), 1.0, 0.0).astype(BF16)
    cum = dot(earlier, sel.astype(BF16))
    code = sel * (cum + 1.0)
    lane512 = iota((32, 512), 1)
    row512 = iota((32, 512), 0)
    spread = jnp.where(lane512 // 16 == row512, 1.0, 0.0).astype(BF16)
    codes = dot(code.astype(BF16), spread)
    want = ((lane512 // 8) % 2 + 1).astype(F32)
    qt = jnp.where((codes == want) & (row512 // 4 == lane512 % 8), 1.0, 0.0)
    qt_s[...] = qt
    q_s[...] = qt.T.astype(BF16)
    res_l[...] = jnp.zeros_like(res_l)
    gain_l[...] = jnp.zeros_like(gain_l)
    d_f[...] = jnp.zeros_like(d_f)
    for k in range(NK):
        res_l[4 * k : 4 * k + 4, :] = res_ref[:, k * CH : (k + 1) * CH].astype(F32)
        gain_l[4 * k : 4 * k + 4, :] = jnp.broadcast_to(gain_ref[k * CH : (k + 1) * CH].reshape(1, CH), (4, CH))

    zeros64 = jnp.zeros((256, 64), F32)
    qr = qr_ref[...].astype(F32)
    q_l[...] = jnp.concatenate([qr, zeros64], axis=1).astype(BF16)
    q_r[...] = jnp.concatenate([zeros64, qr], axis=1).astype(BF16)
    newk[...] = jnp.zeros_like(newk)
    newr[...] = jnp.zeros_like(newr)
    for r in range(2):
        newk[2 * r : 2 * r + 2, :] = nl_ref[r].astype(F32)
        newr[2 * r : 2 * r + 2, 0:64] = nr_ref[r].astype(F32)
    nk = newk[...].astype(BF16)
    s = (dot_nt(q_ref[...], nk) + dot_nt(q_l[...], newr[...].astype(BF16))) * SCORE_SCALE
    row = iota((256, 128), 0)
    col = iota((256, 128), 1)
    ok = (col < 4) & (col // 2 == row // 128) & (col % 2 <= (row // 64) % 2)
    s = jnp.where(ok, s, NEG)
    m = jnp.max(s, -1, keepdims=True)
    p = jnp.exp(s - m)
    m_s[...] = jnp.broadcast_to(m, (256, 128))
    l_s[...] = jnp.broadcast_to(jnp.sum(p, -1, keepdims=True), (256, 128))
    o_s[...] = dot(p.astype(BF16), nk)

    def attend(keys, s_rope, scale, bias0, bias1):
        s = (dot_nt(q_ref[...], keys) + s_rope) * (scale * SCORE_SCALE)
        s = jnp.concatenate([s[:128] + bias0, s[128:] + bias1], axis=0)
        m_old = m_s[:, 0:1]
        m_new = jnp.maximum(m_old, jnp.max(s, -1, keepdims=True))
        p = jnp.exp(s - m_new)
        alpha = jnp.exp(m_old - m_new)
        m_s[...] = jnp.broadcast_to(m_new, (256, 128))
        l_s[...] = jnp.broadcast_to(l_s[:, 0:1] * alpha + jnp.sum(p, -1, keepdims=True), (256, 128))
        o_s[...] = o_s[...] * alpha + dot((p * scale).astype(BF16), keys)

    @pl.loop(0, 12)
    def _(n):
        keys = lat_v[pl.ds(n * 4, 4)].reshape(256, 512)
        ropes = rope_ref[pl.ds(n * 4, 4)].reshape(256, 128)
        sc = [scale_of(n * 4 + m) for m in range(4)]
        scale = jnp.concatenate([jnp.where(low1, sc[0], sc[1]), jnp.where(low1, sc[2], sc[3])], axis=1)
        attend(keys, dot_nt(q_l[...], ropes), scale, bias_of(0, n * 4), bias_of(1, n * 4))

    def attend_moved(k, lat_at, rope_at):
        source = ((x - k // 2 + 4) % 4) * 2 + (c + k % 2) % 2
        v = 48 + source * 4
        ropes = rope_at[0:128, :]
        lo = dot_nt(q_l[...], ropes)
        hi = dot_nt(q_r[...], ropes)
        s_rope = jnp.concatenate([lo[:, :64], hi[:, :64], lo[:, 64:], hi[:, 64:]], axis=1)
        sc = rope_at[128:144, :].astype(F32)
        scale = jnp.concatenate([sc[0:1], sc[1:2]], axis=1)
        attend(lat_at[...], s_rope, scale, bias_of(0, v), bias_of(1, v))

    attend_moved(0, slat.at[0], srope.at[0])

    def moved_from(k):
        page_copy(k, 0).wait_recv()
        page_copy(k, 1).wait_recv()
        attend_moved(k, rlat.at[k], rrope.at[k])

    def pass_on(kind):
        w_copy(kind, 0).wait_recv()
        if kind < 2:
            w_copy(kind, 2).start()
        w_copy(kind, 4).start()
        w_copy(kind, 1).wait_recv()
        if kind < 2:
            w_copy(kind, 3).start()
        w_copy(kind, 5).start()

    pass_on(0)
    moved_from(1)
    pass_on(1)

    @pl.loop(2, 4)
    def _(k):
        moved_from(k)

    pass_on(2)

    @pl.loop(4, 8)
    def _(k):
        moved_from(k)

    o = (o_s[...] / l_s[:, 0:1]).astype(BF16)
    pr = iota((256, 256), 0)
    pc = iota((256, 256), 1)
    source = (pr // 8 % 4) * 64 + ((y + pr // 2 % 4) % 4) * 16 + (pr // 32) * 2 + pr % 2
    perm = jnp.where(pc == source, 1.0, 0.0).astype(BF16)
    so[...] = dot(perm, o).astype(BF16).reshape(8, 32, CH)

    def o_copy(n):
        return rcopy(so.at[(z + n) % 8], ro.at[n], o_ss.at[n], o_rs.at[n], (i, ex_at(0, n)))

    for n in (4, 3, 5, 2, 6, 1, 7):
        o_copy(n).start()
    ro[0] = so[z]
    for kind in range(2):
        w_copy(kind, 2).wait_recv()
        w_copy(kind, 3).wait_recv()
        w_copy(kind, 6).start()
    for n in range(1, 8):
        o_copy(n).wait_recv()

    for n in (4, 5, 6):
        w_copy(0, n).wait_recv()

    wcat = jnp.concatenate([wuv[d, h] for d in range(4) for h in range(2)], axis=1)
    hv = dot(ro[...].reshape(256, CH), wcat)
    hv = jnp.where(iota((256, 1024), 0) % 8 == iota((256, 1024), 1) // 128, hv, 0.0).astype(BF16)
    fr_, fc = iota((32, 256), 0), iota((32, 256), 1)
    fold = jnp.where(fc // 8 == ((z - fr_ // 4 + 8) % 8) * 4 + fr_ % 4, 1.0, 0.0).astype(BF16)
    hv = dot(fold, hv).astype(BF16)
    for kind, n in ((1, 4), (1, 5), (1, 6), (2, 4), (2, 5)):
        w_copy(kind, n).wait_recv()
    for k in range(NK):
        w = slice(k * CH, (k + 1) * CH)
        s_f[:, w] = sum(dot(hv[:, d * 256 : (d + 1) * 256], wout[d, :, w]) for d in range(4))
    for zz in range(8):
        for k in range(NK):
            d_f[zz, 4 * k : 4 * k + 4, :] = s_f[4 * zz : 4 * zz + 4, k * CH : (k + 1) * CH]
    sp2[...] = d_f[...].astype(BF16)

    def z_copy(n):
        zz = (z + n) % 8
        return rcopy(sp2.at[zz], pr2.at[n], p2_s.at[n], p2_r.at[n], (i, ex_at(0, n)))

    for n in (4, 3, 5, 2, 6, 1, 7):
        z_copy(n).start()
    total = d_f[z]
    for n in range(1, 8):
        z_copy(n).wait_recv()
        total = total + pr2[n].astype(F32)
    al_f[...] = total

    hidden = (res_l[...] + total).astype(BF16).astype(F32)
    same = jnp.where(r32 % 4 == e32 % 4, 1.0, 0.0)
    sq = jnp.broadcast_to(jnp.sum(hidden * hidden, -1, keepdims=True), (32, 128))
    sq = jnp.dot(same, sq, precision=lax.Precision.HIGHEST, preferred_element_type=F32)
    normed = (hidden * lax.rsqrt(sq[:, 0:1] / D + NORM_EPS) * gain_l[...]).astype(BF16)
    sd[...] = dot(q_s[...], normed).astype(BF16).reshape(32, 16, CH)

    def d_copy(k):
        e = ex_at(k // 8, k % 8)
        return rcopy(sd.at[e], rd.at[k], d_ss.at[k], d_rs.at[k], (i, e))

    @pl.loop(1, 32)
    def _(k):
        d_copy(k).start()

    rd[0] = sd[j]

    acc = jnp.zeros((32, 32), F32)
    for k in range(NK):
        lg = dot_nt(normed, wr_ref[:, k * CH : (k + 1) * CH])
        acc = acc + jnp.where(r32 // 4 == k, lg, 0.0)
    logits = jnp.dot(same, acc, precision=lax.Precision.HIGHEST, preferred_element_type=F32)
    sig = sel / (1.0 + jnp.exp(-logits))
    gates = ROUTE_SCALE * sig / jnp.sum(sig, -1, keepdims=True)
    g_hi = gates.astype(BF16)
    g_lo = (gates - g_hi.astype(F32)).astype(BF16)
    c_hi = (dot(g_hi, spread) * qt_s[...]).astype(BF16)
    c_lo = (dot(g_lo, spread) * qt_s[...]).astype(BF16)
    for k in range(NK):
        out_ref[0:4, k * CH : (k + 1) * CH] = al_f[4 * k : 4 * k + 4, :].astype(BF16)
    for n in range(16, 19):
        loads[n].wait()

    def ag(g, n):
        lo, hi = pl.ds(0, HALF), pl.ds(HALF, HALF)
        src, dst, dev = [
            (xr.at[g, 0], xr.at[g, 3], right),
            (xr.at[g, 0], xr.at[g, 1], left),
            (xr.at[g, 3, :, lo], xr.at[g, 2, :, lo], right),
            (xr.at[g, 1, :, hi], xr.at[g, 2, :, hi], left),
            (xr.at[g, 0], xr.at[g, 4], sib),
            (xr.at[g, 3], xr.at[g, 7], sib),
            (xr.at[g, 1], xr.at[g, 5], sib),
            (xr.at[g, 2], xr.at[g, 6], sib),
        ][n]
        return rcopy(src, dst, ag_s.at[g, n], ag_r.at[g, n], dev)

    def rs(g, n):
        lo, hi = pl.ds(0, HALF), pl.ds(HALF, HALF)
        src, dst, dev = [
            (pp.at[g, pl.ds(4, 4)], sr.at[g], sib),
            (hb.at[g, :, lo], hr.at[g, 0], right),
            (hb.at[g, :, hi], hr.at[g, 1], left),
            (fb.at[g, 0], fr.at[g, 0], right),
            (fb.at[g, 1], fr.at[g, 1], left),
        ][n]
        return rcopy(src, dst, rs_s.at[g, n], rs_r.at[g, n], dev)

    def b_copy(k):
        e = ex_at(-(k // 8), -(k % 8))
        return rcopy(sret.at[k], rret.at[j], b_ss.at[k], b_rs.at[k], (i, e))

    def stage_a(g):
        @pl.loop(0, 8)
        def _(n):
            @pl.when(g * 8 + n > 0)
            def _():
                d_copy(g * 8 + n).wait_recv()

        got = rd[pl.ds(g * 8, 8)].reshape(128, CH).astype(F32)
        for b in range(4):
            t_f[b * 128 : (b + 1) * 128, :] = got[:, b * 128 : (b + 1) * 128]
        for k in range(NK):
            for b in range(4):
                at = k * CH + b * 128
                xr[g, 0, :, at : at + 128] = t_f[pl.ds(b * 128 + k, 16, stride=8), :].astype(BF16)
        for n in (0, 1, 4):
            ag(g, n).start()

    def stage_b(g):
        ag(g, 0).wait_recv()
        ag(g, 2).start()
        ag(g, 5).start()
        ag(g, 1).wait_recv()
        ag(g, 3).start()
        ag(g, 6).start()

    def stage_c(g):
        ag(g, 2).wait_recv()
        ag(g, 3).wait_recv()
        ag(g, 7).start()
        for n in range(4, 8):
            ag(g, n).wait_recv()

    def stage_d(g):
        rows = xr[g].reshape(128, D)
        gate = dot(rows, wg[...])
        up = dot(rows, wu[...])
        h = (gate / (1.0 + jnp.exp(-gate)) * up).astype(BF16)
        for k in range(NK):
            w = slice(k * CH, (k + 1) * CH)
            pp[g, :, :, w] = dot(h, wd[:, w]).astype(BF16).reshape(8, 16, CH)
        rs(g, 0).start()

    def stage_e(g):
        rs(g, 0).wait_recv()
        ss[g] = pp[g, 0:4].astype(F32) + sr[g].astype(F32)
        hb[g] = ss[g, 2].astype(BF16)
        rs(g, 1).start()
        rs(g, 2).start()

    def stage_f(g):
        rs(g, 1).wait_recv()
        fb[g, 0, :, 0:HALF] = (ss[g, 1, :, 0:HALF] + hr[g, 0].astype(F32)).astype(BF16)
        fb[g, 0, :, HALF:] = ss[g, 1, :, HALF:].astype(BF16)
        rs(g, 3).start()
        rs(g, 2).wait_recv()
        fb[g, 1, :, 0:HALF] = ss[g, 3, :, 0:HALF].astype(BF16)
        fb[g, 1, :, HALF:] = (ss[g, 3, :, HALF:] + hr[g, 1].astype(F32)).astype(BF16)
        rs(g, 4).start()

    def stage_g(g):
        rs(g, 3).wait_recv()
        rs(g, 4).wait_recv()
        for b in range(4):
            for k in range(NK):
                w = slice(k * CH + b * 128, k * CH + b * 128 + 128)
                v = ss[g, 0, :, w] + fr[g, 0, :, w].astype(F32) + fr[g, 1, :, w].astype(F32)
                t_f[pl.ds(b * 128 + k, 16, stride=8), :] = v
            t_f[pl.ds(b * 128 + 7, 16, stride=8), :] = jnp.zeros((16, 128), F32)
        back = jnp.concatenate([t_f[b * 128 : (b + 1) * 128, :] for b in range(4)], axis=1)
        sret[pl.ds(g * 8, 8)] = back.astype(BF16).reshape(8, 16, CH)

        @pl.loop(0, 8)
        def _(n):
            @pl.when(g * 8 + n > 0)
            def _():
                b_copy(g * 8 + n).start()

    stages = [(stage_a, 0), (stage_b, 1), (stage_c, 2), (stage_d, 2), (stage_e, 3), (stage_f, 4), (stage_g, 5)]

    @pl.loop(0, 9)
    def _(t):
        for fn, lag in stages:

            @pl.when((t >= lag) & (t < lag + 4))
            def _(fn=fn, lag=lag):
                fn(t - lag)

    rret[j] = sret[0]

    @pl.loop(1, 32)
    def _(k):
        b_copy(k).wait_recv()

    rows = rret[...].reshape(512, CH)
    al_f[...] = dot(c_hi, rows) + dot(c_lo, rows)
    for k in range(NK):
        out_ref[4:8, k * CH : (k + 1) * CH] = al_f[4 * k : 4 * k + 4, :].astype(BF16)

    @pl.loop(1, 8)
    def _(k):
        page_copy(k, 0).wait_send()
        page_copy(k, 1).wait_send()

    @pl.loop(1, 32)
    def _(k):
        d_copy(k).wait_send()
        b_copy(k).wait_send()

    for kind in range(3):
        for n in range(7):
            if kind < 2 or n in (0, 1, 4, 5):
                w_copy(kind, n).wait_send()
    for n in range(1, 8):
        o_copy(n).wait_send()
        z_copy(n).wait_send()

    @pl.loop(0, 4)
    def _(g):
        for n in range(8):
            ag(g, n).wait_send()
        for n in range(5):
            rs(g, n).wait_send()


def body(
    cache_lat, cache_rope, page_scale, move_list, page_table, lengths, q_lat, q_rope, new_lat, new_rope,
    w_uv, w_out, residual, norm_gain, w_router, routes, w_gate, w_up, w_down,
):
    any_spec = pl.BlockSpec(memory_space=pl.ANY)
    vmem = pl.BlockSpec(memory_space=pltpu.VMEM)
    dma = pltpu.SemaphoreType.DMA
    vm = pltpu.VMEM
    operands = (
        move_list.transpose(0, 2, 1), page_scale, lengths, page_table, cache_lat, cache_rope,
        q_lat.reshape(256, 512), q_rope.reshape(256, 64), new_lat, new_rope, w_uv, w_out, residual,
        norm_gain, w_router.T, routes, w_gate, w_up, w_down,
    )
    out = pl.pallas_call(
        kernel,
        out_shape=jax.ShapeDtypeStruct((8, D), BF16),
        in_specs=[any_spec] * len(operands),
        out_specs=vmem,
        scratch_shapes=[
            pltpu.SMEM((4, 8), jnp.int32), vm((48,), BF16), pltpu.SMEM((2,), jnp.int32), vm((2, 32), jnp.int32),
            vm((48, 4096), BF16), vm((256, 512), BF16), vm((256, 64), BF16), vm((2, 2, 512), BF16), vm((2, 2, 64), BF16),
            vm((4, D), BF16), vm((D,), F32), vm((32, D), BF16), vm((4, 8), jnp.int32),
            vm((48 * 64, 128), F32), vm((48, 64, 128), BF16), vm((2, 80, 128), F32), vm((128, 128), F32), vm((32, 8), jnp.int32),
            vm((48, 64, 512), BF16), vm((4, 2, 512, 128), BF16), vm((4, 256, D), BF16),
            vm((D, 256), BF16), vm((D, 256), BF16), vm((256, D), BF16),
            vm((8, 256, 512), BF16), vm((8, 144, 128), BF16), vm((8, 256, 512), BF16), vm((8, 144, 128), BF16),
            vm((128, 512), F32), vm((128, 128), F32), vm((256, 128), BF16), vm((256, 128), BF16),
            vm((256, 128), F32), vm((256, 128), F32), vm((256, 512), F32),
            vm((8, 32, CH), BF16), vm((8, 32, CH), BF16), vm((32, D), F32),
            vm((8, 32, CH), F32), vm((8, 32, CH), BF16), vm((8, 32, CH), BF16),
            vm((32, CH), F32), vm((32, CH), F32), vm((32, CH), F32),
            vm((512, 32), BF16), vm((32, 512), F32), vm((32, 16, CH), BF16), vm((32, 16, CH), BF16),
            vm((512, 128), F32), vm((4, 8, 16, D), BF16), vm((4, 8, 16, D), BF16), vm((4, 4, 16, D), BF16),
            vm((4, 4, 16, D), F32), vm((4, 16, D), BF16), vm((4, 2, 16, HALF), BF16),
            vm((4, 2, 16, D), BF16), vm((4, 2, 16, D), BF16), vm((32, 16, CH), BF16), vm((32, 16, CH), BF16),
            dma((19,)), dma((2, 8)), dma((2, 8)), dma((3, 7)), dma((3, 7)), dma((8,)), dma((8,)),
            dma((8,)), dma((8,)), dma((32,)), dma((32,)), dma((4, 8)), dma((4, 8)), dma((4, 5)), dma((4, 5)),
            dma((32,)), dma((32,)),
        ],
        compiler_params=pltpu.CompilerParams(
            collective_id=0, has_side_effects=True, vmem_limit_bytes=60 * 2**20
        ),
        name="step",
    )(*operands)
    return out[:4], out[4:]


def solution(mesh):
    both = ("dp", "expert")
    return jax.shard_map(
        body,
        mesh=mesh,
        in_specs=(
            P(both, None, None), P(both, None), P(both), P(both, None, None), P(both, None), P(both),
            P(both, None, None, None), P(both, None, None, None), P(both, None, None), P(both, None, None),
            P("expert", None, None), P("expert", None), P(both, None), P(), P(), P(both, None),
            P("expert", None, "dp"), P("expert", None, "dp"), P("expert", "dp", None),
        ),
        out_specs=(P(both, None), P(both, None)),
        check_vma=False,
    )
```

```python
import jax
import jax.numpy as jnp
from jax import lax
from jax.experimental import pallas as pl
from jax.experimental.pallas import tpu as pltpu
from jax.sharding import PartitionSpec as P

MESH = pl.DeviceIdType.MESH
SCORE_SCALE = 0.07216878364870322
ROUTE_SCALE = 2.5
NORM_EPS = 1e-06
NEG = -1e30
F32 = jnp.float32
BF16 = jnp.bfloat16
D = 3584
CH = 512
NK = 7
HALF = 1792


def dot(a, b):
    return lax.dot_general(a, b, (((1,), (0,)), ((), ())), preferred_element_type=F32)


def dot_nt(a, b):
    return lax.dot_general(a, b, (((1,), (1,)), ((), ())), preferred_element_type=F32)


def iota(shape, dim):
    return lax.broadcasted_iota(jnp.int32, shape, dim)


def kernel(
    mv_hbm, ps_hbm, len_hbm, pt_hbm, lat_hbm, rope_hbm, q_hbm, qr_hbm, nl_hbm, nr_hbm,
    wuv_hbm, wout_hbm, res_hbm, gain_hbm, wr_hbm, rt_hbm, wg_hbm, wu_hbm, wd_hbm,
    out_ref,
    mv_ref, ps_ref, len_ref, pt_ref, rope_raw, q_ref, qr_ref, nl_ref, nr_ref, res_ref, gain_ref, wr_ref, rt_ref,
    rope_f, rope_ref, bias_s, scale_s, rt_s,
    lat_v, wuv, wout, wg, wu, wd,
    slat, srope, rlat, rrope, newk, newr, q_l, q_r, m_s, l_s, o_s,
    so, ro, s_f, d_f, sp2, pr2, al_f, res_l, gain_l,
    q_s, qt_s, c_s, sd, rd, t_f, xr, pp, sr, ss, hb, hr, fb, fr, sret, rret,
    lsem, pg_s, pg_r, w_ss, w_rs, o_ss, o_rs, p2_s, p2_r, d_ss, d_rs, ag_s, ag_r, rs_s, rs_r, b_ss, b_rs, met,
):
    i = lax.axis_index("dp")
    j = lax.axis_index("expert")
    x, c, y, z = i // 2, i % 2, j // 8, j % 8

    def dp_to(dx, dc):
        return (((x + dx) % 4) * 2 + (c + dc) % 2, j)

    def ex_at(dy, dz):
        return ((y + dy + 4) % 4) * 8 + (z + dz + 8) % 8

    def rcopy(src, dst, send, recv, dev):
        return pltpu.make_async_remote_copy(
            src_ref=src, dst_ref=dst, send_sem=send, recv_sem=recv, device_id=dev, device_id_type=MESH
        )

    right, left, sib = dp_to(1, 0), dp_to(3, 0), dp_to(0, 1)
    barrier = pltpu.get_barrier_semaphore()

    @pl.loop(1, 8)
    def _(k):
        pl.semaphore_signal(barrier, inc=1, device_id=dp_to(k // 2, k % 2), device_id_type=MESH)

    near = ((1, 0), (-1, 0), (0, 1), (0, -1))
    for dy, dz in near:
        pl.semaphore_signal(barrier, inc=1, device_id=(i, ex_at(dy, dz)), device_id_type=MESH)

    rounds = (near, ((0, 2), (0, -2)), ((0, 4), (0, 1), (0, -1)))

    def tell(n):
        for dy, dz in rounds[n]:
            pl.semaphore_signal(met.at[n], inc=1, device_id=(i, ex_at(dy, dz)), device_id_type=MESH)

    def hear(n):
        pl.semaphore_wait(met.at[n], len(rounds[n]))

    pairs = [
        (mv_hbm.at[0], mv_ref), (lat_hbm, lat_v), (wuv_hbm, wuv.at[0]), (wout_hbm, wout.at[0]), (ps_hbm, ps_ref),
        (rope_hbm, rope_raw), (len_hbm, len_ref), (pt_hbm, pt_ref), (q_hbm, q_ref), (qr_hbm, qr_ref),
        (nl_hbm, nl_ref), (nr_hbm, nr_ref), (rt_hbm, rt_ref), (res_hbm, res_ref), (gain_hbm, gain_ref),
        (wr_hbm, wr_ref), (wg_hbm.at[0], wg), (wu_hbm.at[0], wu), (wd_hbm.at[0], wd),
    ]
    loads = [pltpu.make_async_copy(a, b, lsem.at[n]) for n, (a, b) in enumerate(pairs)]
    for cp in loads[:16]:
        cp.start()

    loads[0].wait()
    loads[1].wait()

    def dest_of(k):
        return ((x + k // 2) % 4) * 2 + (c + k % 2) % 2

    @pl.loop(0, 8)
    def _(k):
        dest = dest_of(k)
        for m in range(4):
            slat[k, m * 64 : (m + 1) * 64, :] = lat_v[mv_ref[m, dest]]

    def page_copy(k, n):
        dev = dp_to(k // 2, k % 2)
        if n == 0:
            return rcopy(slat.at[k], rlat.at[k], pg_s.at[0, k], pg_r.at[0, k], dev)
        return rcopy(srope.at[k], rrope.at[k], pg_s.at[1, k], pg_r.at[1, k], dev)

    up_y, down_y = (i, ex_at(1, 0)), (i, ex_at(-1, 0))

    def w_copy(kind, n):
        if kind == 0:
            own = [wuv.at[d, c] for d in range(4)]
            up = [wuv.at[d, c, pl.ds(0, 256)] for d in range(4)]
            down = [wuv.at[d, c, pl.ds(256, 256)] for d in range(4)]
            near_up = near_down = own
        else:
            rows = pl.ds(c * 128, 128)
            own = [wout.at[d, rows] for d in range(4)]
            up = [wout.at[d, rows, pl.ds(0, HALF)] for d in range(4)]
            down = [wout.at[d, rows, pl.ds(HALF, HALF)] for d in range(4)]
            near_up, near_down = (up, down) if kind == 1 else (down, up)
        src, dst, dev = [
            (near_up[0], near_up[3], up_y),
            (near_down[0], near_down[1], down_y),
            (up[3], up[2], up_y),
            (down[1], down[2], down_y),
            (near_up[3], near_up[3], sib),
            (near_down[1], near_down[1], sib),
            (own[2], own[2], sib),
        ][n]
        return rcopy(src, dst, w_ss.at[kind, n], w_rs.at[kind, n], dev)

    pl.semaphore_wait(barrier, 11)
    tell(0)

    loads[2].wait()
    loads[3].wait()
    for kind in range(3):
        w_copy(kind, 0).start()
        w_copy(kind, 1).start()
    for k in (4, 5, 2, 6, 3, 7, 1):
        page_copy(k, 0).start()
    for cp in loads[16:]:
        cp.start()

    hear(0)
    tell(1)

    loads[4].wait()
    loads[5].wait()
    low48 = iota((48, 128), 1) < 64
    for g in range(32):
        v = rope_raw[:, g * 128 : (g + 1) * 128].astype(F32)
        w = pltpu.roll(v, 64, axis=1)
        rope_f[pl.ds(2 * g, 48, stride=64), :] = jnp.where(low48, v, w)
        rope_f[pl.ds(2 * g + 1, 48, stride=64), :] = jnp.where(low48, w, v)

    @pl.loop(0, 48)
    def _(n):
        rope_ref[n] = rope_f[pl.ds(pl.multiple_of(n * 64, 64), 64), :].astype(BF16)

    scales = jnp.concatenate([ps_ref[...].astype(F32).reshape(1, 48), jnp.zeros((1, 80), F32)], axis=1)
    scale_s[...] = jnp.broadcast_to(scales, (128, 128)).T

    def scale_of(v):
        return scale_s[pl.ds(v, 1), :]

    low_lane = iota((64, 128), 1) < 64
    low16 = iota((16, 128), 1) < 64
    row16 = iota((16, 128), 0)

    @pl.loop(0, 8)
    def _(k):
        dest = dest_of(k)
        pages = [mv_ref[m, dest] for m in range(4)]
        for m in range(2):
            a = rope_ref[pages[2 * m]].astype(F32)
            b = rope_ref[pages[2 * m + 1]].astype(F32)
            srope[k, m * 64 : (m + 1) * 64, :] = jnp.where(low_lane, a, b).astype(BF16)
        scales = [scale_of(pages[m]) for m in range(4)]
        first = jnp.where(low16, scales[0], scales[1])
        second = jnp.where(low16, scales[2], scales[3])
        srope[k, 128:144, :] = jnp.where(row16 == 0, first, second).astype(BF16)

    for k in (4, 5, 2, 6, 3, 7, 1):
        page_copy(k, 1).start()

    hear(1)
    tell(2)

    for n in range(6, 16):
        loads[n].wait()
    page_id = iota((80, 32), 0)
    entry = iota((80, 32), 1)
    in_page = iota((80, 128), 1) % 64
    for r in range(2):
        fits = jnp.where(pt_ref[r : r + 1, :] == page_id, len_ref[r] - entry * 64, 0)
        limit = jnp.max(fits, axis=1, keepdims=True)
        bias_s[r] = jnp.where(in_page < limit, 0.0, NEG)
    low1 = iota((1, 128), 1) < 64

    def bias_of(r, v):
        b = [bias_s[r, pl.ds(v + m, 1), :] for m in range(4)]
        return jnp.concatenate([jnp.where(low1, b[0], b[1]), jnp.where(low1, b[2], b[3])], axis=1)

    for k in range(8):
        rt_s[4 * k : 4 * k + 4, :] = rt_ref[...]
    e32 = iota((32, 32), 1)
    sel = jnp.zeros((32, 32), F32)
    for kk in range(8):
        sel = jnp.where(rt_s[:, kk : kk + 1] == e32, 1.0, sel)
    r32 = iota((32, 32), 0)
    earlier = jnp.where((r32 // 4 == e32 // 4) & (e32 % 4 < r32 % 4), 1.0, 0.0).astype(BF16)
    cum = dot(earlier, sel.astype(BF16))
    code = sel * (cum + 1.0)
    lane512 = iota((32, 512), 1)
    row512 = iota((32, 512), 0)
    spread = jnp.where(lane512 // 16 == row512, 1.0, 0.0).astype(BF16)
    codes = dot(code.astype(BF16), spread)
    want = ((lane512 // 8) % 2 + 1).astype(F32)
    qt = jnp.where((codes == want) & (row512 // 4 == lane512 % 8), 1.0, 0.0)
    qt_s[...] = qt
    q_s[...] = qt.T.astype(BF16)
    res_l[...] = jnp.zeros_like(res_l)
    gain_l[...] = jnp.zeros_like(gain_l)
    d_f[...] = jnp.zeros_like(d_f)
    for k in range(NK):
        res_l[4 * k : 4 * k + 4, :] = res_ref[:, k * CH : (k + 1) * CH].astype(F32)
        gain_l[4 * k : 4 * k + 4, :] = jnp.broadcast_to(gain_ref[k * CH : (k + 1) * CH].reshape(1, CH), (4, CH))

    hear(2)

    zeros64 = jnp.zeros((256, 64), F32)
    qr = qr_ref[...].astype(F32)
    q_l[...] = jnp.concatenate([qr, zeros64], axis=1).astype(BF16)
    q_r[...] = jnp.concatenate([zeros64, qr], axis=1).astype(BF16)
    newk[...] = jnp.zeros_like(newk)
    newr[...] = jnp.zeros_like(newr)
    for r in range(2):
        newk[2 * r : 2 * r + 2, :] = nl_ref[r].astype(F32)
        newr[2 * r : 2 * r + 2, 0:64] = nr_ref[r].astype(F32)
    nk = newk[...].astype(BF16)
    s = (dot_nt(q_ref[...], nk) + dot_nt(q_l[...], newr[...].astype(BF16))) * SCORE_SCALE
    row = iota((256, 128), 0)
    col = iota((256, 128), 1)
    ok = (col < 4) & (col // 2 == row // 128) & (col % 2 <= (row // 64) % 2)
    s = jnp.where(ok, s, NEG)
    m = jnp.max(s, -1, keepdims=True)
    p = jnp.exp(s - m)
    m_s[...] = jnp.broadcast_to(m, (256, 128))
    l_s[...] = jnp.broadcast_to(jnp.sum(p, -1, keepdims=True), (256, 128))
    o_s[...] = dot(p.astype(BF16), nk)

    def attend(keys, s_rope, scale, bias0, bias1):
        s = (dot_nt(q_ref[...], keys) + s_rope) * (scale * SCORE_SCALE)
        s = jnp.concatenate([s[:128] + bias0, s[128:] + bias1], axis=0)
        m_old = m_s[:, 0:1]
        m_new = jnp.maximum(m_old, jnp.max(s, -1, keepdims=True))
        p = jnp.exp(s - m_new)
        alpha = jnp.exp(m_old - m_new)
        m_s[...] = jnp.broadcast_to(m_new, (256, 128))
        l_s[...] = jnp.broadcast_to(l_s[:, 0:1] * alpha + jnp.sum(p, -1, keepdims=True), (256, 128))
        o_s[...] = o_s[...] * alpha + dot((p * scale).astype(BF16), keys)

    @pl.loop(0, 12)
    def _(n):
        keys = lat_v[pl.ds(n * 4, 4)].reshape(256, 512)
        ropes = rope_ref[pl.ds(n * 4, 4)].reshape(256, 128)
        sc = [scale_of(n * 4 + m) for m in range(4)]
        scale = jnp.concatenate([jnp.where(low1, sc[0], sc[1]), jnp.where(low1, sc[2], sc[3])], axis=1)
        attend(keys, dot_nt(q_l[...], ropes), scale, bias_of(0, n * 4), bias_of(1, n * 4))

    def attend_moved(k, lat_at, rope_at):
        source = ((x - k // 2 + 4) % 4) * 2 + (c + k % 2) % 2
        v = 48 + source * 4
        ropes = rope_at[0:128, :]
        lo = dot_nt(q_l[...], ropes)
        hi = dot_nt(q_r[...], ropes)
        s_rope = jnp.concatenate([lo[:, :64], hi[:, :64], lo[:, 64:], hi[:, 64:]], axis=1)
        sc = rope_at[128:144, :].astype(F32)
        scale = jnp.concatenate([sc[0:1], sc[1:2]], axis=1)
        attend(lat_at[...], s_rope, scale, bias_of(0, v), bias_of(1, v))

    attend_moved(0, slat.at[0], srope.at[0])

    def moved_from(k):
        page_copy(k, 0).wait_recv()
        page_copy(k, 1).wait_recv()
        attend_moved(k, rlat.at[k], rrope.at[k])

    def pass_on(kind):
        w_copy(kind, 0).wait_recv()
        if kind < 2:
            w_copy(kind, 2).start()
        w_copy(kind, 4).start()
        w_copy(kind, 1).wait_recv()
        if kind < 2:
            w_copy(kind, 3).start()
        w_copy(kind, 5).start()

    pass_on(0)
    moved_from(1)
    pass_on(1)

    @pl.loop(4, 6)
    def _(k):
        moved_from(k)

    pass_on(2)

    @pl.loop(0, 4)
    def _(n):
        moved_from(2 + (n % 2) * 4 + n // 2)

    o = (o_s[...] / l_s[:, 0:1]).astype(BF16)
    pr = iota((256, 256), 0)
    pc = iota((256, 256), 1)
    source = (pr // 8 % 4) * 64 + ((y + pr // 2 % 4) % 4) * 16 + (pr // 32) * 2 + pr % 2
    perm = jnp.where(pc == source, 1.0, 0.0).astype(BF16)
    so[...] = dot(perm, o).astype(BF16).reshape(8, 32, CH)

    def o_copy(n):
        return rcopy(so.at[(z + n) % 8], ro.at[n], o_ss.at[n], o_rs.at[n], (i, ex_at(0, n)))

    for n in (4, 3, 5, 2, 6, 1, 7):
        o_copy(n).start()
    ro[0] = so[z]
    for kind in range(2):
        w_copy(kind, 2).wait_recv()
        w_copy(kind, 3).wait_recv()
        w_copy(kind, 6).start()
    for n in range(1, 8):
        o_copy(n).wait_recv()

    for n in (4, 5, 6):
        w_copy(0, n).wait_recv()

    wcat = jnp.concatenate([wuv[d, h] for d in range(4) for h in range(2)], axis=1)
    hv = dot(ro[...].reshape(256, CH), wcat)
    hv = jnp.where(iota((256, 1024), 0) % 8 == iota((256, 1024), 1) // 128, hv, 0.0).astype(BF16)
    fr_, fc = iota((32, 256), 0), iota((32, 256), 1)
    fold = jnp.where(fc // 8 == ((z - fr_ // 4 + 8) % 8) * 4 + fr_ % 4, 1.0, 0.0).astype(BF16)
    hv = dot(fold, hv).astype(BF16)
    for kind, n in ((1, 4), (1, 5), (1, 6), (2, 4), (2, 5)):
        w_copy(kind, n).wait_recv()
    def z_copy(n, part):
        rows = pl.ds(part * 16, 16)
        return rcopy(
            sp2.at[(z + n) % 8, rows], pr2.at[n, rows], p2_s.at[part, n], p2_r.at[part, n], (i, ex_at(0, n))
        )

    far_first = (4, 3, 5, 2, 6, 1, 7)
    for part in range(2):
        for k in range(4 * part, min(4 * part + 4, NK)):
            w = slice(k * CH, (k + 1) * CH)
            s_f[:, w] = sum(dot(hv[:, d * 256 : (d + 1) * 256], wout[d, :, w]) for d in range(4))
            for zz in range(8):
                d_f[zz, 4 * k : 4 * k + 4, :] = s_f[4 * zz : 4 * zz + 4, w]
        sp2[:, 16 * part : 16 * part + 16, :] = d_f[:, 16 * part : 16 * part + 16, :].astype(BF16)
        for n in far_first:
            z_copy(n, part).start()
    total = d_f[z]
    for n in range(1, 8):
        z_copy(n, 0).wait_recv()
        z_copy(n, 1).wait_recv()
        total = total + pr2[n].astype(F32)
    al_f[...] = total

    hidden = (res_l[...] + total).astype(BF16).astype(F32)
    same = jnp.where(r32 % 4 == e32 % 4, 1.0, 0.0)
    sq = jnp.broadcast_to(jnp.sum(hidden * hidden, -1, keepdims=True), (32, 128))
    sq = jnp.dot(same, sq, precision=lax.Precision.HIGHEST, preferred_element_type=F32)
    normed = (hidden * lax.rsqrt(sq[:, 0:1] / D + NORM_EPS) * gain_l[...]).astype(BF16)
    sd[...] = dot(q_s[...], normed).astype(BF16).reshape(32, 16, CH)

    def d_copy(k):
        e = ex_at(k // 8, k % 8)
        return rcopy(sd.at[e], rd.at[k], d_ss.at[k], d_rs.at[k], (i, e))

    @pl.loop(1, 32)
    def _(k):
        d_copy(k).start()

    rd[0] = sd[j]

    acc = jnp.zeros((32, 32), F32)
    for k in range(NK):
        lg = dot_nt(normed, wr_ref[:, k * CH : (k + 1) * CH])
        acc = acc + jnp.where(r32 // 4 == k, lg, 0.0)
    logits = jnp.dot(same, acc, precision=lax.Precision.HIGHEST, preferred_element_type=F32)
    sig = sel / (1.0 + jnp.exp(-logits))
    gates = ROUTE_SCALE * sig / jnp.sum(sig, -1, keepdims=True)
    g_hi = gates.astype(BF16)
    g_lo = (gates - g_hi.astype(F32)).astype(BF16)
    c_s[0] = (dot(g_hi, spread) * qt_s[...]).astype(BF16)
    c_s[1] = (dot(g_lo, spread) * qt_s[...]).astype(BF16)
    for k in range(NK):
        out_ref[0:4, k * CH : (k + 1) * CH] = al_f[4 * k : 4 * k + 4, :].astype(BF16)
    for n in range(16, 19):
        loads[n].wait()

    def ag(g, n):
        lo, hi = pl.ds(0, HALF), pl.ds(HALF, HALF)
        src, dst, dev = [
            (xr.at[g, 0], xr.at[g, 3], right),
            (xr.at[g, 0], xr.at[g, 1], left),
            (xr.at[g, 3, :, lo], xr.at[g, 2, :, lo], right),
            (xr.at[g, 1, :, hi], xr.at[g, 2, :, hi], left),
            (xr.at[g, 0], xr.at[g, 4], sib),
            (xr.at[g, 3], xr.at[g, 7], sib),
            (xr.at[g, 1], xr.at[g, 5], sib),
            (xr.at[g, 2], xr.at[g, 6], sib),
        ][n]
        return rcopy(src, dst, ag_s.at[g, n], ag_r.at[g, n], dev)

    def rs(g, n):
        lo, hi = pl.ds(0, HALF), pl.ds(HALF, HALF)
        src, dst, dev = [
            (pp.at[g, pl.ds(4, 4)], sr.at[g], sib),
            (hb.at[g, :, lo], hr.at[g, 0], right),
            (hb.at[g, :, hi], hr.at[g, 1], left),
            (fb.at[g, 0], fr.at[g, 0], right),
            (fb.at[g, 1], fr.at[g, 1], left),
        ][n]
        return rcopy(src, dst, rs_s.at[g, n], rs_r.at[g, n], dev)

    def b_copy(k):
        e = ex_at(-(k // 8), -(k % 8))
        return rcopy(sret.at[k], rret.at[j], b_ss.at[k], b_rs.at[k], (i, e))

    def stage_a(g):
        @pl.loop(0, 8)
        def _(n):
            @pl.when(g * 8 + n > 0)
            def _():
                d_copy(g * 8 + n).wait_recv()

        got = rd[pl.ds(g * 8, 8)].reshape(128, CH).astype(F32)
        for b in range(4):
            t_f[b * 128 : (b + 1) * 128, :] = got[:, b * 128 : (b + 1) * 128]
        for k in range(NK):
            for b in range(4):
                at = k * CH + b * 128
                xr[g, 0, :, at : at + 128] = t_f[pl.ds(b * 128 + k, 16, stride=8), :].astype(BF16)
        for n in (0, 1, 4):
            ag(g, n).start()

    def stage_b(g):
        ag(g, 0).wait_recv()
        ag(g, 2).start()
        ag(g, 5).start()
        ag(g, 1).wait_recv()
        ag(g, 3).start()
        ag(g, 6).start()

    def stage_c(g):
        ag(g, 2).wait_recv()
        ag(g, 3).wait_recv()
        ag(g, 7).start()
        for n in range(4, 8):
            ag(g, n).wait_recv()

    def stage_d(g):
        rows = xr[g].reshape(128, D)
        gate = dot(rows, wg[...])
        up = dot(rows, wu[...])
        h = (gate / (1.0 + jnp.exp(-gate)) * up).astype(BF16)
        for k in range(NK):
            w = slice(k * CH, (k + 1) * CH)
            pp[g, :, :, w] = dot(h, wd[:, w]).astype(BF16).reshape(8, 16, CH)
        rs(g, 0).start()

    def stage_e(g):
        rs(g, 0).wait_recv()
        ss[g] = pp[g, 0:4].astype(F32) + sr[g].astype(F32)
        hb[g] = ss[g, 2].astype(BF16)
        rs(g, 1).start()
        rs(g, 2).start()

    def stage_f(g):
        rs(g, 1).wait_recv()
        fb[g, 0, :, 0:HALF] = (ss[g, 1, :, 0:HALF] + hr[g, 0].astype(F32)).astype(BF16)
        fb[g, 0, :, HALF:] = ss[g, 1, :, HALF:].astype(BF16)
        rs(g, 3).start()
        rs(g, 2).wait_recv()
        fb[g, 1, :, 0:HALF] = ss[g, 3, :, 0:HALF].astype(BF16)
        fb[g, 1, :, HALF:] = (ss[g, 3, :, HALF:] + hr[g, 1].astype(F32)).astype(BF16)
        rs(g, 4).start()

    def stage_g(g):
        rs(g, 3).wait_recv()
        rs(g, 4).wait_recv()
        for b in range(4):
            for k in range(NK):
                w = slice(k * CH + b * 128, k * CH + b * 128 + 128)
                v = ss[g, 0, :, w] + fr[g, 0, :, w].astype(F32) + fr[g, 1, :, w].astype(F32)
                t_f[pl.ds(b * 128 + k, 16, stride=8), :] = v
            t_f[pl.ds(b * 128 + 7, 16, stride=8), :] = jnp.zeros((16, 128), F32)
        back = jnp.concatenate([t_f[b * 128 : (b + 1) * 128, :] for b in range(4)], axis=1)
        sret[pl.ds(g * 8, 8)] = back.astype(BF16).reshape(8, 16, CH)

        @pl.loop(0, 8)
        def _(n):
            @pl.when(g * 8 + n > 0)
            def _():
                b_copy(g * 8 + n).start()

    stages = [(stage_a, 0), (stage_b, 1), (stage_c, 2), (stage_d, 2), (stage_e, 3), (stage_f, 4), (stage_g, 5)]

    @pl.loop(0, 9)
    def _(t):
        for fn, lag in stages:

            @pl.when((t >= lag) & (t < lag + 4))
            def _(fn=fn, lag=lag):
                fn(t - lag)

    rret[j] = sret[0]

    @pl.loop(1, 8)
    def _(k):
        page_copy(k, 0).wait_send()
        page_copy(k, 1).wait_send()

    for kind in range(3):
        for n in range(7):
            if kind < 2 or n in (0, 1, 4, 5):
                w_copy(kind, n).wait_send()
    for n in range(1, 8):
        o_copy(n).wait_send()
        z_copy(n, 0).wait_send()
        z_copy(n, 1).wait_send()

    @pl.loop(0, 4)
    def _(g):
        for n in range(8):
            ag(g, n).wait_send()
        for n in range(5):
            rs(g, n).wait_send()

    @pl.loop(1, 32)
    def _(k):
        d_copy(k).wait_send()
        b_copy(k).wait_send()

    al_f[...] = jnp.zeros_like(al_f)
    for g in range(4):
        for n in range(8):
            if g * 8 + n:
                b_copy(g * 8 + n).wait_recv()
        group = (y + g) % 4
        rows = rret[pl.ds(group * 8, 8)].reshape(128, CH)
        lanes = pl.ds(pl.multiple_of(group * 128, 128), 128)
        al_f[...] += dot(c_s[0, :, lanes], rows) + dot(c_s[1, :, lanes], rows)
    for k in range(NK):
        out_ref[4:8, k * CH : (k + 1) * CH] = al_f[4 * k : 4 * k + 4, :].astype(BF16)


def body(
    cache_lat, cache_rope, page_scale, move_list, page_table, lengths, q_lat, q_rope, new_lat, new_rope,
    w_uv, w_out, residual, norm_gain, w_router, routes, w_gate, w_up, w_down,
):
    any_spec = pl.BlockSpec(memory_space=pl.ANY)
    vmem = pl.BlockSpec(memory_space=pltpu.VMEM)
    dma = pltpu.SemaphoreType.DMA
    vm = pltpu.VMEM
    operands = (
        move_list.transpose(0, 2, 1), page_scale, lengths, page_table, cache_lat, cache_rope,
        q_lat.reshape(256, 512), q_rope.reshape(256, 64), new_lat, new_rope, w_uv, w_out, residual,
        norm_gain, w_router.T, routes, w_gate, w_up, w_down,
    )
    out = pl.pallas_call(
        kernel,
        out_shape=jax.ShapeDtypeStruct((8, D), BF16),
        in_specs=[any_spec] * len(operands),
        out_specs=vmem,
        scratch_shapes=[
            pltpu.SMEM((4, 8), jnp.int32), vm((48,), BF16), pltpu.SMEM((2,), jnp.int32), vm((2, 32), jnp.int32),
            vm((48, 4096), BF16), vm((256, 512), BF16), vm((256, 64), BF16), vm((2, 2, 512), BF16), vm((2, 2, 64), BF16),
            vm((4, D), BF16), vm((D,), F32), vm((32, D), BF16), vm((4, 8), jnp.int32),
            vm((48 * 64, 128), F32), vm((48, 64, 128), BF16), vm((2, 80, 128), F32), vm((128, 128), F32), vm((32, 8), jnp.int32),
            vm((48, 64, 512), BF16), vm((4, 2, 512, 128), BF16), vm((4, 256, D), BF16),
            vm((D, 256), BF16), vm((D, 256), BF16), vm((256, D), BF16),
            vm((8, 256, 512), BF16), vm((8, 144, 128), BF16), vm((8, 256, 512), BF16), vm((8, 144, 128), BF16),
            vm((128, 512), F32), vm((128, 128), F32), vm((256, 128), BF16), vm((256, 128), BF16),
            vm((256, 128), F32), vm((256, 128), F32), vm((256, 512), F32),
            vm((8, 32, CH), BF16), vm((8, 32, CH), BF16), vm((32, D), F32),
            vm((8, 32, CH), F32), vm((8, 32, CH), BF16), vm((8, 32, CH), BF16),
            vm((32, CH), F32), vm((32, CH), F32), vm((32, CH), F32),
            vm((512, 32), BF16), vm((32, 512), F32), vm((2, 32, 512), BF16), vm((32, 16, CH), BF16), vm((32, 16, CH), BF16),
            vm((512, 128), F32), vm((4, 8, 16, D), BF16), vm((4, 8, 16, D), BF16), vm((4, 4, 16, D), BF16),
            vm((4, 4, 16, D), F32), vm((4, 16, D), BF16), vm((4, 2, 16, HALF), BF16),
            vm((4, 2, 16, D), BF16), vm((4, 2, 16, D), BF16), vm((32, 16, CH), BF16), vm((32, 16, CH), BF16),
            dma((19,)), dma((2, 8)), dma((2, 8)), dma((3, 7)), dma((3, 7)), dma((8,)), dma((8,)),
            dma((2, 8)), dma((2, 8)), dma((32,)), dma((32,)), dma((4, 8)), dma((4, 8)), dma((4, 5)), dma((4, 5)),
            dma((32,)), dma((32,)), pltpu.SemaphoreType.REGULAR((3,)),
        ],
        compiler_params=pltpu.CompilerParams(
            collective_id=0, has_side_effects=True, vmem_limit_bytes=60 * 2**20
        ),
        name="step",
    )(*operands)
    return out[:4], out[4:]


def solution(mesh):
    both = ("dp", "expert")
    return jax.shard_map(
        body,
        mesh=mesh,
        in_specs=(
            P(both, None, None), P(both, None), P(both), P(both, None, None), P(both, None), P(both),
            P(both, None, None, None), P(both, None, None, None), P(both, None, None), P(both, None, None),
            P("expert", None, None), P("expert", None), P(both, None), P(), P(), P(both, None),
            P("expert", None, "dp"), P("expert", None, "dp"), P("expert", "dp", None),
        ),
        out_specs=(P(both, None), P(both, None)),
        check_vma=False,
    )
```

```python
import jax
import jax.numpy as jnp
from jax import lax
from jax.experimental import pallas as pl
from jax.experimental.pallas import tpu as pltpu
from jax.sharding import PartitionSpec as P

MESH = pl.DeviceIdType.MESH
SCORE_SCALE = 0.07216878364870322
ROUTE_SCALE = 2.5
NORM_EPS = 1e-06
NEG = -1e30
F32 = jnp.float32
BF16 = jnp.bfloat16
D = 3584
CH = 512
NK = 7
HALF = 1792


def dot(a, b):
    return lax.dot_general(a, b, (((1,), (0,)), ((), ())), preferred_element_type=F32)


def dot_nt(a, b):
    return lax.dot_general(a, b, (((1,), (1,)), ((), ())), preferred_element_type=F32)


def iota(shape, dim):
    return lax.broadcasted_iota(jnp.int32, shape, dim)


def kernel(
    mv_hbm, ps_hbm, len_hbm, pt_hbm, lat_hbm, rope_hbm, q_hbm, qr_hbm, nl_hbm, nr_hbm,
    wuv_hbm, wout_hbm, res_hbm, gain_hbm, wr_hbm, rt_hbm, wg_hbm, wu_hbm, wd_hbm,
    out_ref,
    mv_ref, ps_ref, len_ref, pt_ref, rope_raw, q_ref, qr_ref, nl_ref, nr_ref, res_ref, gain_ref, wr_ref, rt_ref,
    rope_f, rope_ref, bias_s, scale_s, rt_s,
    lat_v, wuv, wout, wg, wu, wd,
    slat, srope, rlat, rrope, newk, newr, q_l, q_r, m_s, l_s, o_s,
    so, ro, s_f, d_f, sp2, pr2, al_f, res_l, gain_l,
    q_s, qt_s, c_s, sd, rd, t_f, xr, pp, sr, ss, hb, hr, fb, fr, sret, rret,
    lsem, pg_s, pg_r, w_ss, w_rs, o_ss, o_rs, p2_s, p2_r, d_ss, d_rs, ag_s, ag_r, rs_s, rs_r, b_ss, b_rs, met,
):
    i = lax.axis_index("dp")
    j = lax.axis_index("expert")
    x, c, y, z = i // 2, i % 2, j // 8, j % 8

    def dp_to(dx, dc):
        return (((x + dx) % 4) * 2 + (c + dc) % 2, j)

    def ex_at(dy, dz):
        return ((y + dy + 4) % 4) * 8 + (z + dz + 8) % 8

    def rcopy(src, dst, send, recv, dev):
        return pltpu.make_async_remote_copy(
            src_ref=src, dst_ref=dst, send_sem=send, recv_sem=recv, device_id=dev, device_id_type=MESH
        )

    right, left, sib = dp_to(1, 0), dp_to(3, 0), dp_to(0, 1)
    barrier = pltpu.get_barrier_semaphore()

    @pl.loop(1, 8)
    def _(k):
        pl.semaphore_signal(barrier, inc=1, device_id=dp_to(k // 2, k % 2), device_id_type=MESH)

    near = ((1, 0), (-1, 0), (0, 1), (0, -1))
    for dy, dz in near:
        pl.semaphore_signal(barrier, inc=1, device_id=(i, ex_at(dy, dz)), device_id_type=MESH)

    rounds = (near, ((0, 2), (0, -2)), ((0, 4), (0, 1), (0, -1)))

    def tell(n):
        for dy, dz in rounds[n]:
            pl.semaphore_signal(met.at[n], inc=1, device_id=(i, ex_at(dy, dz)), device_id_type=MESH)

    def hear(n):
        pl.semaphore_wait(met.at[n], len(rounds[n]))

    pairs = [
        (mv_hbm.at[0], mv_ref), (lat_hbm, lat_v), (wuv_hbm, wuv.at[0]), (wout_hbm, wout.at[0]), (ps_hbm, ps_ref),
        (rope_hbm, rope_raw), (len_hbm, len_ref), (pt_hbm, pt_ref), (q_hbm, q_ref), (qr_hbm, qr_ref),
        (nl_hbm, nl_ref), (nr_hbm, nr_ref), (rt_hbm, rt_ref), (res_hbm, res_ref), (gain_hbm, gain_ref),
        (wr_hbm, wr_ref), (wg_hbm.at[0], wg), (wu_hbm.at[0], wu), (wd_hbm.at[0], wd),
    ]
    loads = [pltpu.make_async_copy(a, b, lsem.at[n]) for n, (a, b) in enumerate(pairs)]
    for cp in loads[:16]:
        cp.start()

    loads[0].wait()
    loads[1].wait()

    def dest_of(k):
        return ((x + k // 2) % 4) * 2 + (c + k % 2) % 2

    @pl.loop(0, 8)
    def _(k):
        dest = dest_of(k)
        for m in range(4):
            slat[k, m * 64 : (m + 1) * 64, :] = lat_v[mv_ref[m, dest]]

    def page_copy(k, n):
        dev = dp_to(k // 2, k % 2)
        if n == 0:
            return rcopy(slat.at[k], rlat.at[k], pg_s.at[0, k], pg_r.at[0, k], dev)
        return rcopy(srope.at[k], rrope.at[k], pg_s.at[1, k], pg_r.at[1, k], dev)

    up_y, down_y = (i, ex_at(1, 0)), (i, ex_at(-1, 0))

    def w_copy(kind, n):
        if kind == 0:
            own = [wuv.at[d, c] for d in range(4)]
            up = [wuv.at[d, c, pl.ds(0, 256)] for d in range(4)]
            down = [wuv.at[d, c, pl.ds(256, 256)] for d in range(4)]
            near_up = near_down = own
        else:
            rows = pl.ds(c * 128, 128)
            own = [wout.at[d, rows] for d in range(4)]
            up = [wout.at[d, rows, pl.ds(0, HALF)] for d in range(4)]
            down = [wout.at[d, rows, pl.ds(HALF, HALF)] for d in range(4)]
            near_up, near_down = (up, down) if kind == 1 else (down, up)
        src, dst, dev = [
            (near_up[0], near_up[3], up_y),
            (near_down[0], near_down[1], down_y),
            (up[3], up[2], up_y),
            (down[1], down[2], down_y),
            (near_up[3], near_up[3], sib),
            (near_down[1], near_down[1], sib),
            (own[2], own[2], sib),
        ][n]
        return rcopy(src, dst, w_ss.at[kind, n], w_rs.at[kind, n], dev)

    pl.semaphore_wait(barrier, 11)
    tell(0)

    loads[2].wait()
    loads[3].wait()
    for kind in range(3):
        w_copy(kind, 0).start()
        w_copy(kind, 1).start()
    page_copy(4, 0).start()
    page_copy(5, 0).start()
    for cp in loads[16:]:
        cp.start()

    hear(0)
    tell(1)

    loads[4].wait()
    loads[5].wait()
    low48 = iota((48, 128), 1) < 64
    for g in range(32):
        v = rope_raw[:, g * 128 : (g + 1) * 128].astype(F32)
        w = pltpu.roll(v, 64, axis=1)
        rope_f[pl.ds(2 * g, 48, stride=64), :] = jnp.where(low48, v, w)
        rope_f[pl.ds(2 * g + 1, 48, stride=64), :] = jnp.where(low48, w, v)

    @pl.loop(0, 48)
    def _(n):
        rope_ref[n] = rope_f[pl.ds(pl.multiple_of(n * 64, 64), 64), :].astype(BF16)

    scales = jnp.concatenate([ps_ref[...].astype(F32).reshape(1, 48), jnp.zeros((1, 80), F32)], axis=1)
    scale_s[...] = jnp.broadcast_to(scales, (128, 128)).T

    def scale_of(v):
        return scale_s[pl.ds(v, 1), :]

    low_lane = iota((64, 128), 1) < 64
    low16 = iota((16, 128), 1) < 64
    row16 = iota((16, 128), 0)

    @pl.loop(0, 8)
    def _(k):
        dest = dest_of(k)
        pages = [mv_ref[m, dest] for m in range(4)]
        for m in range(2):
            a = rope_ref[pages[2 * m]].astype(F32)
            b = rope_ref[pages[2 * m + 1]].astype(F32)
            srope[k, m * 64 : (m + 1) * 64, :] = jnp.where(low_lane, a, b).astype(BF16)
        scales = [scale_of(pages[m]) for m in range(4)]
        first = jnp.where(low16, scales[0], scales[1])
        second = jnp.where(low16, scales[2], scales[3])
        srope[k, 128:144, :] = jnp.where(row16 == 0, first, second).astype(BF16)

    page_copy(4, 1).start()
    page_copy(5, 1).start()
    for k in (2, 6, 3, 7, 1):
        page_copy(k, 0).start()
        page_copy(k, 1).start()

    hear(1)
    tell(2)

    for n in range(6, 16):
        loads[n].wait()
    page_id = iota((80, 32), 0)
    entry = iota((80, 32), 1)
    in_page = iota((80, 128), 1) % 64
    for r in range(2):
        fits = jnp.where(pt_ref[r : r + 1, :] == page_id, len_ref[r] - entry * 64, 0)
        limit = jnp.max(fits, axis=1, keepdims=True)
        bias_s[r] = jnp.where(in_page < limit, 0.0, NEG)
    low1 = iota((1, 128), 1) < 64

    def bias_of(r, v):
        b = [bias_s[r, pl.ds(v + m, 1), :] for m in range(4)]
        return jnp.concatenate([jnp.where(low1, b[0], b[1]), jnp.where(low1, b[2], b[3])], axis=1)

    for k in range(8):
        rt_s[4 * k : 4 * k + 4, :] = rt_ref[...]
    e32 = iota((32, 32), 1)
    sel = jnp.zeros((32, 32), F32)
    for kk in range(8):
        sel = jnp.where(rt_s[:, kk : kk + 1] == e32, 1.0, sel)
    r32 = iota((32, 32), 0)
    earlier = jnp.where((r32 // 4 == e32 // 4) & (e32 % 4 < r32 % 4), 1.0, 0.0).astype(BF16)
    cum = dot(earlier, sel.astype(BF16))
    code = sel * (cum + 1.0)
    lane512 = iota((32, 512), 1)
    row512 = iota((32, 512), 0)
    spread = jnp.where(lane512 // 16 == row512, 1.0, 0.0).astype(BF16)
    codes = dot(code.astype(BF16), spread)
    want = ((lane512 // 8) % 2 + 1).astype(F32)
    qt = jnp.where((codes == want) & (row512 // 4 == lane512 % 8), 1.0, 0.0)
    qt_s[...] = qt
    q_s[...] = qt.T.astype(BF16)
    res_l[...] = jnp.zeros_like(res_l)
    gain_l[...] = jnp.zeros_like(gain_l)
    d_f[...] = jnp.zeros_like(d_f)
    for k in range(NK):
        res_l[4 * k : 4 * k + 4, :] = res_ref[:, k * CH : (k + 1) * CH].astype(F32)
        gain_l[4 * k : 4 * k + 4, :] = jnp.broadcast_to(gain_ref[k * CH : (k + 1) * CH].reshape(1, CH), (4, CH))

    hear(2)

    zeros64 = jnp.zeros((256, 64), F32)
    qr = qr_ref[...].astype(F32)
    q_l[...] = jnp.concatenate([qr, zeros64], axis=1).astype(BF16)
    q_r[...] = jnp.concatenate([zeros64, qr], axis=1).astype(BF16)
    newk[...] = jnp.zeros_like(newk)
    newr[...] = jnp.zeros_like(newr)
    for r in range(2):
        newk[2 * r : 2 * r + 2, :] = nl_ref[r].astype(F32)
        newr[2 * r : 2 * r + 2, 0:64] = nr_ref[r].astype(F32)
    nk = newk[...].astype(BF16)
    s = (dot_nt(q_ref[...], nk) + dot_nt(q_l[...], newr[...].astype(BF16))) * SCORE_SCALE
    row = iota((256, 128), 0)
    col = iota((256, 128), 1)
    ok = (col < 4) & (col // 2 == row // 128) & (col % 2 <= (row // 64) % 2)
    s = jnp.where(ok, s, NEG)
    m = jnp.max(s, -1, keepdims=True)
    p = jnp.exp(s - m)
    m_s[...] = jnp.broadcast_to(m, (256, 128))
    l_s[...] = jnp.broadcast_to(jnp.sum(p, -1, keepdims=True), (256, 128))
    o_s[...] = dot(p.astype(BF16), nk)

    def attend(keys, s_rope, scale, bias0, bias1):
        s = (dot_nt(q_ref[...], keys) + s_rope) * (scale * SCORE_SCALE)
        s = jnp.concatenate([s[:128] + bias0, s[128:] + bias1], axis=0)
        m_old = m_s[:, 0:1]
        m_new = jnp.maximum(m_old, jnp.max(s, -1, keepdims=True))
        p = jnp.exp(s - m_new)
        alpha = jnp.exp(m_old - m_new)
        m_s[...] = jnp.broadcast_to(m_new, (256, 128))
        l_s[...] = jnp.broadcast_to(l_s[:, 0:1] * alpha + jnp.sum(p, -1, keepdims=True), (256, 128))
        o_s[...] = o_s[...] * alpha + dot((p * scale).astype(BF16), keys)

    @pl.loop(0, 12)
    def _(n):
        keys = lat_v[pl.ds(n * 4, 4)].reshape(256, 512)
        ropes = rope_ref[pl.ds(n * 4, 4)].reshape(256, 128)
        sc = [scale_of(n * 4 + m) for m in range(4)]
        scale = jnp.concatenate([jnp.where(low1, sc[0], sc[1]), jnp.where(low1, sc[2], sc[3])], axis=1)
        attend(keys, dot_nt(q_l[...], ropes), scale, bias_of(0, n * 4), bias_of(1, n * 4))

    def attend_moved(k, lat_at, rope_at):
        source = ((x - k // 2 + 4) % 4) * 2 + (c + k % 2) % 2
        v = 48 + source * 4
        ropes = rope_at[0:128, :]
        lo = dot_nt(q_l[...], ropes)
        hi = dot_nt(q_r[...], ropes)
        s_rope = jnp.concatenate([lo[:, :64], hi[:, :64], lo[:, 64:], hi[:, 64:]], axis=1)
        sc = rope_at[128:144, :].astype(F32)
        scale = jnp.concatenate([sc[0:1], sc[1:2]], axis=1)
        attend(lat_at[...], s_rope, scale, bias_of(0, v), bias_of(1, v))

    attend_moved(0, slat.at[0], srope.at[0])

    def moved_from(k):
        page_copy(k, 0).wait_recv()
        page_copy(k, 1).wait_recv()
        attend_moved(k, rlat.at[k], rrope.at[k])

    def pass_on(kind):
        w_copy(kind, 0).wait_recv()
        if kind < 2:
            w_copy(kind, 2).start()
        w_copy(kind, 4).start()
        w_copy(kind, 1).wait_recv()
        if kind < 2:
            w_copy(kind, 3).start()
        w_copy(kind, 5).start()

    pass_on(0)
    pass_on(1)

    @pl.loop(4, 6)
    def _(k):
        moved_from(k)

    pass_on(2)

    moved_from(1)

    @pl.loop(0, 4)
    def _(n):
        moved_from(2 + (n % 2) * 4 + n // 2)

    o = (o_s[...] / l_s[:, 0:1]).astype(BF16)
    pr = iota((256, 256), 0)
    pc = iota((256, 256), 1)
    source = (pr // 8 % 4) * 64 + ((y + pr // 2 % 4) % 4) * 16 + (pr // 32) * 2 + pr % 2
    perm = jnp.where(pc == source, 1.0, 0.0).astype(BF16)
    so[...] = dot(perm, o).astype(BF16).reshape(8, 32, CH)

    def o_copy(n):
        return rcopy(so.at[(z + n) % 8], ro.at[n], o_ss.at[n], o_rs.at[n], (i, ex_at(0, n)))

    for n in (4, 3, 5, 2, 6, 1, 7):
        o_copy(n).start()
    ro[0] = so[z]
    for kind in range(2):
        w_copy(kind, 2).wait_recv()
        w_copy(kind, 3).wait_recv()
        w_copy(kind, 6).start()
    for n in range(1, 8):
        o_copy(n).wait_recv()

    for n in (4, 5, 6):
        w_copy(0, n).wait_recv()

    wcat = jnp.concatenate([wuv[d, h] for d in range(4) for h in range(2)], axis=1)
    hv = dot(ro[...].reshape(256, CH), wcat)
    hv = jnp.where(iota((256, 1024), 0) % 8 == iota((256, 1024), 1) // 128, hv, 0.0).astype(BF16)
    fr_, fc = iota((32, 256), 0), iota((32, 256), 1)
    fold = jnp.where(fc // 8 == ((z - fr_ // 4 + 8) % 8) * 4 + fr_ % 4, 1.0, 0.0).astype(BF16)
    hv = dot(fold, hv).astype(BF16)
    for kind, n in ((1, 4), (1, 5), (1, 6), (2, 4), (2, 5)):
        w_copy(kind, n).wait_recv()
    def z_copy(n, part):
        rows = pl.ds(part * 16, 16)
        return rcopy(
            sp2.at[(z + n) % 8, rows], pr2.at[n, rows], p2_s.at[part, n], p2_r.at[part, n], (i, ex_at(0, n))
        )

    far_first = (4, 3, 5, 2, 6, 1, 7)
    for part in range(2):
        for k in range(4 * part, min(4 * part + 4, NK)):
            w = slice(k * CH, (k + 1) * CH)
            s_f[:, w] = sum(dot(hv[:, d * 256 : (d + 1) * 256], wout[d, :, w]) for d in range(4))
            for zz in range(8):
                d_f[zz, 4 * k : 4 * k + 4, :] = s_f[4 * zz : 4 * zz + 4, w]
        sp2[:, 16 * part : 16 * part + 16, :] = d_f[:, 16 * part : 16 * part + 16, :].astype(BF16)
        for n in far_first:
            z_copy(n, part).start()
    total = d_f[z]
    for n in range(1, 8):
        z_copy(n, 0).wait_recv()
        z_copy(n, 1).wait_recv()
        total = total + pr2[n].astype(F32)
    al_f[...] = total

    hidden = (res_l[...] + total).astype(BF16).astype(F32)
    same = jnp.where(r32 % 4 == e32 % 4, 1.0, 0.0)
    sq = jnp.broadcast_to(jnp.sum(hidden * hidden, -1, keepdims=True), (32, 128))
    sq = jnp.dot(same, sq, precision=lax.Precision.HIGHEST, preferred_element_type=F32)
    normed = (hidden * lax.rsqrt(sq[:, 0:1] / D + NORM_EPS) * gain_l[...]).astype(BF16)
    sd[...] = dot(q_s[...], normed).astype(BF16).reshape(32, 16, CH)

    def d_copy(k):
        e = ex_at(k // 8, k % 8)
        return rcopy(sd.at[e], rd.at[k], d_ss.at[k], d_rs.at[k], (i, e))

    for dy in range(4):
        for dz in (4, 3, 5, 2, 6, 1, 7, 0):
            if dy or dz:
                d_copy(dy * 8 + dz).start()

    rd[0] = sd[j]

    acc = jnp.zeros((32, 32), F32)
    for k in range(NK):
        lg = dot_nt(normed, wr_ref[:, k * CH : (k + 1) * CH])
        acc = acc + jnp.where(r32 // 4 == k, lg, 0.0)
    logits = jnp.dot(same, acc, precision=lax.Precision.HIGHEST, preferred_element_type=F32)
    sig = sel / (1.0 + jnp.exp(-logits))
    gates = ROUTE_SCALE * sig / jnp.sum(sig, -1, keepdims=True)
    g_hi = gates.astype(BF16)
    g_lo = (gates - g_hi.astype(F32)).astype(BF16)
    c_s[0] = (dot(g_hi, spread) * qt_s[...]).astype(BF16)
    c_s[1] = (dot(g_lo, spread) * qt_s[...]).astype(BF16)
    for k in range(NK):
        out_ref[0:4, k * CH : (k + 1) * CH] = al_f[4 * k : 4 * k + 4, :].astype(BF16)
    for n in range(16, 19):
        loads[n].wait()

    def ag(g, n):
        lo, hi = pl.ds(0, HALF), pl.ds(HALF, HALF)
        src, dst, dev = [
            (xr.at[g, 0, :, lo], xr.at[g, 3, :, lo], right),
            (xr.at[g, 0, :, hi], xr.at[g, 1, :, hi], left),
            (xr.at[g, 3, :, lo], xr.at[g, 2, :, lo], right),
            (xr.at[g, 1, :, hi], xr.at[g, 2, :, hi], left),
            (xr.at[g, 0], xr.at[g, 4], sib),
            (xr.at[g, 3], xr.at[g, 7], sib),
            (xr.at[g, 1], xr.at[g, 5], sib),
            (xr.at[g, 2], xr.at[g, 6], sib),
            (xr.at[g, 0, :, hi], xr.at[g, 3, :, hi], right),
            (xr.at[g, 0, :, lo], xr.at[g, 1, :, lo], left),
        ][n]
        return rcopy(src, dst, ag_s.at[g, n], ag_r.at[g, n], dev)

    def rs(g, n):
        lo, hi = pl.ds(0, HALF), pl.ds(HALF, HALF)
        src, dst, dev = [
            (pp.at[g, pl.ds(4, 4)], sr.at[g], sib),
            (hb.at[g, :, lo], hr.at[g, 0], right),
            (hb.at[g, :, hi], hr.at[g, 1], left),
            (fb.at[g, 0, :, hi], fr.at[g, 0, :, hi], right),
            (fb.at[g, 1, :, lo], fr.at[g, 1, :, lo], left),
            (fb.at[g, 0, :, lo], fr.at[g, 0, :, lo], right),
            (fb.at[g, 1, :, hi], fr.at[g, 1, :, hi], left),
        ][n]
        return rcopy(src, dst, rs_s.at[g, n], rs_r.at[g, n], dev)

    def b_copy(k):
        e = ex_at(-(k // 8), -(k % 8))
        return rcopy(sret.at[k], rret.at[j], b_ss.at[k], b_rs.at[k], (i, e))

    def stage_a(g):
        @pl.loop(0, 8)
        def _(n):
            @pl.when(g * 8 + n > 0)
            def _():
                d_copy(g * 8 + n).wait_recv()

        got = rd[pl.ds(g * 8, 8)].reshape(128, CH).astype(F32)
        for b in range(4):
            t_f[b * 128 : (b + 1) * 128, :] = got[:, b * 128 : (b + 1) * 128]
        for k in range(NK):
            for b in range(4):
                at = k * CH + b * 128
                xr[g, 0, :, at : at + 128] = t_f[pl.ds(b * 128 + k, 16, stride=8), :].astype(BF16)
        for n in (0, 1, 8, 9, 4):
            ag(g, n).start()

    def stage_b(g):
        ag(g, 0).wait_recv()
        ag(g, 2).start()
        ag(g, 1).wait_recv()
        ag(g, 3).start()
        ag(g, 8).wait_recv()
        ag(g, 5).start()
        ag(g, 9).wait_recv()
        ag(g, 6).start()

    def stage_c(g):
        ag(g, 2).wait_recv()
        ag(g, 3).wait_recv()
        ag(g, 7).start()
        for n in range(4, 8):
            ag(g, n).wait_recv()

    def stage_d(g):
        rows = xr[g].reshape(128, D)
        gate = dot(rows, wg[...])
        up = dot(rows, wu[...])
        h = (gate / (1.0 + jnp.exp(-gate)) * up).astype(BF16)
        for k in range(NK):
            w = slice(k * CH, (k + 1) * CH)
            pp[g, :, :, w] = dot(h, wd[:, w]).astype(BF16).reshape(8, 16, CH)
        rs(g, 0).start()

    def stage_e(g):
        rs(g, 0).wait_recv()
        hb[g] = (pp[g, 2].astype(F32) + sr[g, 2].astype(F32)).astype(BF16)
        rs(g, 1).start()
        rs(g, 2).start()
        ss[g] = pp[g, 0:4].astype(F32) + sr[g].astype(F32)
        fb[g, 0, :, HALF:] = ss[g, 1, :, HALF:].astype(BF16)
        fb[g, 1, :, 0:HALF] = ss[g, 3, :, 0:HALF].astype(BF16)
        rs(g, 3).start()
        rs(g, 4).start()

    def stage_f(g):
        rs(g, 1).wait_recv()
        fb[g, 0, :, 0:HALF] = (ss[g, 1, :, 0:HALF] + hr[g, 0].astype(F32)).astype(BF16)
        rs(g, 5).start()
        rs(g, 2).wait_recv()
        fb[g, 1, :, HALF:] = (ss[g, 3, :, HALF:] + hr[g, 1].astype(F32)).astype(BF16)
        rs(g, 6).start()

    def stage_g(g):
        for n in range(3, 7):
            rs(g, n).wait_recv()
        for b in range(4):
            for k in range(NK):
                w = slice(k * CH + b * 128, k * CH + b * 128 + 128)
                v = ss[g, 0, :, w] + fr[g, 0, :, w].astype(F32) + fr[g, 1, :, w].astype(F32)
                t_f[pl.ds(b * 128 + k, 16, stride=8), :] = v
            t_f[pl.ds(b * 128 + 7, 16, stride=8), :] = jnp.zeros((16, 128), F32)
        back = jnp.concatenate([t_f[b * 128 : (b + 1) * 128, :] for b in range(4)], axis=1)
        sret[pl.ds(g * 8, 8)] = back.astype(BF16).reshape(8, 16, CH)

        for n in (4, 3, 5, 2, 6, 1, 7):
            b_copy(g * 8 + n).start()

        @pl.when(g > 0)
        def _():
            b_copy(g * 8).start()

    stages = [(stage_a, 0), (stage_b, 1), (stage_c, 2), (stage_d, 2), (stage_e, 3), (stage_f, 4), (stage_g, 5)]

    @pl.loop(0, 9)
    def _(t):
        for fn, lag in stages:

            @pl.when((t >= lag) & (t < lag + 4))
            def _(fn=fn, lag=lag):
                fn(t - lag)

    rret[j] = sret[0]

    @pl.loop(1, 8)
    def _(k):
        page_copy(k, 0).wait_send()
        page_copy(k, 1).wait_send()

    for kind in range(3):
        for n in range(7):
            if kind < 2 or n in (0, 1, 4, 5):
                w_copy(kind, n).wait_send()
    for n in range(1, 8):
        o_copy(n).wait_send()
        z_copy(n, 0).wait_send()
        z_copy(n, 1).wait_send()

    @pl.loop(0, 4)
    def _(g):
        for n in range(10):
            ag(g, n).wait_send()
        for n in range(7):
            rs(g, n).wait_send()

    @pl.loop(1, 32)
    def _(k):
        d_copy(k).wait_send()
        b_copy(k).wait_send()

    al_f[...] = jnp.zeros_like(al_f)
    for g in range(4):
        for n in range(8):
            if g * 8 + n:
                b_copy(g * 8 + n).wait_recv()
        group = (y + g) % 4
        rows = rret[pl.ds(group * 8, 8)].reshape(128, CH)
        lanes = pl.ds(pl.multiple_of(group * 128, 128), 128)
        al_f[...] += dot(c_s[0, :, lanes], rows) + dot(c_s[1, :, lanes], rows)
    for k in range(NK):
        out_ref[4:8, k * CH : (k + 1) * CH] = al_f[4 * k : 4 * k + 4, :].astype(BF16)


def body(
    cache_lat, cache_rope, page_scale, move_list, page_table, lengths, q_lat, q_rope, new_lat, new_rope,
    w_uv, w_out, residual, norm_gain, w_router, routes, w_gate, w_up, w_down,
):
    any_spec = pl.BlockSpec(memory_space=pl.ANY)
    vmem = pl.BlockSpec(memory_space=pltpu.VMEM)
    dma = pltpu.SemaphoreType.DMA
    vm = pltpu.VMEM
    operands = (
        move_list.transpose(0, 2, 1), page_scale, lengths, page_table, cache_lat, cache_rope,
        q_lat.reshape(256, 512), q_rope.reshape(256, 64), new_lat, new_rope, w_uv, w_out, residual,
        norm_gain, w_router.T, routes, w_gate, w_up, w_down,
    )
    out = pl.pallas_call(
        kernel,
        out_shape=pltpu.VMEM((8, D), BF16),
        in_specs=[any_spec] * len(operands),
        out_specs=vmem,
        scratch_shapes=[
            pltpu.SMEM((4, 8), jnp.int32), vm((48,), BF16), pltpu.SMEM((2,), jnp.int32), vm((2, 32), jnp.int32),
            vm((48, 4096), BF16), vm((256, 512), BF16), vm((256, 64), BF16), vm((2, 2, 512), BF16), vm((2, 2, 64), BF16),
            vm((4, D), BF16), vm((D,), F32), vm((32, D), BF16), vm((4, 8), jnp.int32),
            vm((48 * 64, 128), F32), vm((48, 64, 128), BF16), vm((2, 80, 128), F32), vm((128, 128), F32), vm((32, 8), jnp.int32),
            vm((48, 64, 512), BF16), vm((4, 2, 512, 128), BF16), vm((4, 256, D), BF16),
            vm((D, 256), BF16), vm((D, 256), BF16), vm((256, D), BF16),
            vm((8, 256, 512), BF16), vm((8, 144, 128), BF16), vm((8, 256, 512), BF16), vm((8, 144, 128), BF16),
            vm((128, 512), F32), vm((128, 128), F32), vm((256, 128), BF16), vm((256, 128), BF16),
            vm((256, 128), F32), vm((256, 128), F32), vm((256, 512), F32),
            vm((8, 32, CH), BF16), vm((8, 32, CH), BF16), vm((32, D), F32),
            vm((8, 32, CH), F32), vm((8, 32, CH), BF16), vm((8, 32, CH), BF16),
            vm((32, CH), F32), vm((32, CH), F32), vm((32, CH), F32),
            vm((512, 32), BF16), vm((32, 512), F32), vm((2, 32, 512), BF16), vm((32, 16, CH), BF16), vm((32, 16, CH), BF16),
            vm((512, 128), F32), vm((4, 8, 16, D), BF16), vm((4, 8, 16, D), BF16), vm((4, 4, 16, D), BF16),
            vm((4, 4, 16, D), F32), vm((4, 16, D), BF16), vm((4, 2, 16, HALF), BF16),
            vm((4, 2, 16, D), BF16), vm((4, 2, 16, D), BF16), vm((32, 16, CH), BF16), vm((32, 16, CH), BF16),
            dma((19,)), dma((2, 8)), dma((2, 8)), dma((3, 7)), dma((3, 7)), dma((8,)), dma((8,)),
            dma((2, 8)), dma((2, 8)), dma((32,)), dma((32,)), dma((4, 10)), dma((4, 10)), dma((4, 7)), dma((4, 7)),
            dma((32,)), dma((32,)), pltpu.SemaphoreType.REGULAR((3,)),
        ],
        compiler_params=pltpu.CompilerParams(
            collective_id=0, has_side_effects=True, vmem_limit_bytes=60 * 2**20
        ),
        name="step",
    )(*operands)
    return out[:4], out[4:]


def solution(mesh):
    both = ("dp", "expert")
    return jax.shard_map(
        body,
        mesh=mesh,
        in_specs=(
            P(both, None, None), P(both, None), P(both), P(both, None, None), P(both, None), P(both),
            P(both, None, None, None), P(both, None, None, None), P(both, None, None), P(both, None, None),
            P("expert", None, None), P("expert", None), P(both, None), P(), P(), P(both, None),
            P("expert", None, "dp"), P("expert", None, "dp"), P("expert", "dp", None),
        ),
        out_specs=(P(both, None), P(both, None)),
        check_vma=False,
    )
```

```python
import jax
import jax.numpy as jnp
from jax import lax
from jax.experimental import pallas as pl
from jax.experimental.pallas import tpu as pltpu
from jax.sharding import PartitionSpec as P

MESH = pl.DeviceIdType.MESH
SCORE_SCALE = 0.07216878364870322
ROUTE_SCALE = 2.5
NORM_EPS = 1e-06
NEG = -1e30
F32 = jnp.float32
BF16 = jnp.bfloat16
D = 3584
CH = 512
NK = 7
HALF = 1792


def dot(a, b):
    return lax.dot_general(a, b, (((1,), (0,)), ((), ())), preferred_element_type=F32)


def dot_nt(a, b):
    return lax.dot_general(a, b, (((1,), (1,)), ((), ())), preferred_element_type=F32)


def iota(shape, dim):
    return lax.broadcasted_iota(jnp.int32, shape, dim)


def kernel(
    mv_hbm, ps_hbm, len_hbm, pt_hbm, lat_hbm, rope_hbm, q_hbm, qr_hbm, nl_hbm, nr_hbm,
    wuv_hbm, wout_hbm, res_hbm, gain_hbm, wr_hbm, rt_hbm, wg_hbm, wu_hbm, wd_hbm,
    out_ref,
    mv_ref, ps_ref, len_ref, pt_ref, rope_raw, q_ref, qr_ref, nl_ref, nr_ref, res_ref, gain_ref, wr_ref, rt_ref,
    rope_f, rope_ref, bias_s, scale_s, rt_s,
    lat_v, wuv, wout, wg, wu, wd,
    slat, srope, rlat, rrope, newk, newr, q_l, q_r, m_s, l_s, o_s,
    so, ro, s_f, d_f, sp2, pr2, al_f, res_l, gain_l,
    q_s, qt_s, c_s, sd, rd, t_f, xr, pp, sr, ss, hb, hr, fb, fr, sret, rret,
    lsem, pg_s, pg_r, w_ss, w_rs, o_ss, o_rs, p2_s, p2_r, d_ss, d_rs, ag_s, ag_r, rs_s, rs_r, b_ss, b_rs, met,
):
    i = lax.axis_index("dp")
    j = lax.axis_index("expert")
    x, c, y, z = i // 2, i % 2, j // 8, j % 8

    def dp_to(dx, dc):
        return (((x + dx) % 4) * 2 + (c + dc) % 2, j)

    def ex_at(dy, dz):
        return ((y + dy + 4) % 4) * 8 + (z + dz + 8) % 8

    def rcopy(src, dst, send, recv, dev):
        return pltpu.make_async_remote_copy(
            src_ref=src, dst_ref=dst, send_sem=send, recv_sem=recv, device_id=dev, device_id_type=MESH
        )

    right, left, sib = dp_to(1, 0), dp_to(3, 0), dp_to(0, 1)
    barrier = pltpu.get_barrier_semaphore()

    @pl.loop(1, 8)
    def _(k):
        pl.semaphore_signal(barrier, inc=1, device_id=dp_to(k // 2, k % 2), device_id_type=MESH)

    near = ((1, 0), (-1, 0), (0, 1), (0, -1))
    for dy, dz in near:
        pl.semaphore_signal(barrier, inc=1, device_id=(i, ex_at(dy, dz)), device_id_type=MESH)

    rounds = (near, ((0, 2), (0, -2)), ((0, 4), (0, 1), (0, -1)))

    def tell(n):
        for dy, dz in rounds[n]:
            pl.semaphore_signal(met.at[n], inc=1, device_id=(i, ex_at(dy, dz)), device_id_type=MESH)

    def hear(n):
        pl.semaphore_wait(met.at[n], len(rounds[n]))

    pairs = [
        (mv_hbm.at[0], mv_ref), (lat_hbm, lat_v), (wuv_hbm, wuv.at[0]), (wout_hbm, wout.at[0]), (ps_hbm, ps_ref),
        (rope_hbm, rope_raw), (len_hbm, len_ref), (pt_hbm, pt_ref), (q_hbm, q_ref), (qr_hbm, qr_ref),
        (nl_hbm, nl_ref), (nr_hbm, nr_ref), (rt_hbm, rt_ref), (res_hbm, res_ref), (gain_hbm, gain_ref),
        (wr_hbm, wr_ref), (wg_hbm.at[0], wg), (wu_hbm.at[0], wu), (wd_hbm.at[0], wd),
    ]
    loads = [pltpu.make_async_copy(a, b, lsem.at[n]) for n, (a, b) in enumerate(pairs)]
    for cp in loads[:16]:
        cp.start()

    loads[0].wait()
    loads[1].wait()

    def dest_of(k):
        return ((x + k // 2) % 4) * 2 + (c + k % 2) % 2

    @pl.loop(0, 8)
    def _(k):
        dest = dest_of(k)
        for m in range(4):
            slat[k, m * 64 : (m + 1) * 64, :] = lat_v[mv_ref[m, dest]]

    def page_copy(k, n):
        dev = dp_to(k // 2, k % 2)
        if n == 0:
            return rcopy(slat.at[k], rlat.at[k], pg_s.at[0, k], pg_r.at[0, k], dev)
        return rcopy(srope.at[k], rrope.at[k], pg_s.at[1, k], pg_r.at[1, k], dev)

    up_y, down_y = (i, ex_at(1, 0)), (i, ex_at(-1, 0))

    def w_copy(kind, n):
        if kind == 0:
            own = [wuv.at[d, c] for d in range(4)]
            up = [wuv.at[d, c, pl.ds(0, 256)] for d in range(4)]
            down = [wuv.at[d, c, pl.ds(256, 256)] for d in range(4)]
            near_up = near_down = own
        else:
            rows = pl.ds(c * 128, 128)
            own = [wout.at[d, rows] for d in range(4)]
            up = [wout.at[d, rows, pl.ds(0, HALF)] for d in range(4)]
            down = [wout.at[d, rows, pl.ds(HALF, HALF)] for d in range(4)]
            near_up, near_down = (up, down) if kind == 1 else (down, up)
        src, dst, dev = [
            (near_up[0], near_up[3], up_y),
            (near_down[0], near_down[1], down_y),
            (up[3], up[2], up_y),
            (down[1], down[2], down_y),
            (near_up[3], near_up[3], sib),
            (near_down[1], near_down[1], sib),
            (own[2], own[2], sib),
        ][n]
        return rcopy(src, dst, w_ss.at[kind, n], w_rs.at[kind, n], dev)

    pl.semaphore_wait(barrier, 11)
    tell(0)

    page_copy(4, 0).start()
    page_copy(5, 0).start()
    loads[2].wait()
    loads[3].wait()
    for kind in range(3):
        w_copy(kind, 0).start()
        w_copy(kind, 1).start()
    for cp in loads[16:]:
        cp.start()

    hear(0)
    tell(1)

    loads[4].wait()
    loads[5].wait()
    low48 = iota((48, 128), 1) < 64
    for g in range(32):
        v = rope_raw[:, g * 128 : (g + 1) * 128].astype(F32)
        w = pltpu.roll(v, 64, axis=1)
        rope_f[pl.ds(2 * g, 48, stride=64), :] = jnp.where(low48, v, w)
        rope_f[pl.ds(2 * g + 1, 48, stride=64), :] = jnp.where(low48, w, v)

    @pl.loop(0, 48)
    def _(n):
        rope_ref[n] = rope_f[pl.ds(pl.multiple_of(n * 64, 64), 64), :].astype(BF16)

    scales = jnp.concatenate([ps_ref[...].astype(F32).reshape(1, 48), jnp.zeros((1, 80), F32)], axis=1)
    scale_s[...] = jnp.broadcast_to(scales, (128, 128)).T

    def scale_of(v):
        return scale_s[pl.ds(v, 1), :]

    low_lane = iota((64, 128), 1) < 64
    low16 = iota((16, 128), 1) < 64
    row16 = iota((16, 128), 0)

    @pl.loop(0, 8)
    def _(k):
        dest = dest_of(k)
        pages = [mv_ref[m, dest] for m in range(4)]
        for m in range(2):
            a = rope_ref[pages[2 * m]].astype(F32)
            b = rope_ref[pages[2 * m + 1]].astype(F32)
            srope[k, m * 64 : (m + 1) * 64, :] = jnp.where(low_lane, a, b).astype(BF16)
        scales = [scale_of(pages[m]) for m in range(4)]
        first = jnp.where(low16, scales[0], scales[1])
        second = jnp.where(low16, scales[2], scales[3])
        srope[k, 128:144, :] = jnp.where(row16 == 0, first, second).astype(BF16)

    page_copy(4, 1).start()
    page_copy(5, 1).start()
    for k in (2, 6, 3, 7, 1):
        page_copy(k, 0).start()
        page_copy(k, 1).start()

    hear(1)
    tell(2)

    for n in range(6, 16):
        loads[n].wait()
    page_id = iota((80, 32), 0)
    entry = iota((80, 32), 1)
    in_page = iota((80, 128), 1) % 64
    for r in range(2):
        fits = jnp.where(pt_ref[r : r + 1, :] == page_id, len_ref[r] - entry * 64, 0)
        limit = jnp.max(fits, axis=1, keepdims=True)
        bias_s[r] = jnp.where(in_page < limit, 0.0, NEG)
    low1 = iota((1, 128), 1) < 64

    def bias_of(r, v):
        b = [bias_s[r, pl.ds(v + m, 1), :] for m in range(4)]
        return jnp.concatenate([jnp.where(low1, b[0], b[1]), jnp.where(low1, b[2], b[3])], axis=1)

    for k in range(8):
        rt_s[4 * k : 4 * k + 4, :] = rt_ref[...]
    e32 = iota((32, 32), 1)
    sel = jnp.zeros((32, 32), F32)
    for kk in range(8):
        sel = jnp.where(rt_s[:, kk : kk + 1] == e32, 1.0, sel)
    r32 = iota((32, 32), 0)
    earlier = jnp.where((r32 // 4 == e32 // 4) & (e32 % 4 < r32 % 4), 1.0, 0.0).astype(BF16)
    cum = dot(earlier, sel.astype(BF16))
    code = sel * (cum + 1.0)
    lane512 = iota((32, 512), 1)
    row512 = iota((32, 512), 0)
    spread = jnp.where(lane512 // 16 == row512, 1.0, 0.0).astype(BF16)
    codes = dot(code.astype(BF16), spread)
    want = ((lane512 // 8) % 2 + 1).astype(F32)
    qt = jnp.where((codes == want) & (row512 // 4 == lane512 % 8), 1.0, 0.0)
    qt_s[...] = qt
    q_s[...] = qt.T.astype(BF16)
    res_l[...] = jnp.zeros_like(res_l)
    gain_l[...] = jnp.zeros_like(gain_l)
    d_f[...] = jnp.zeros_like(d_f)
    for k in range(NK):
        res_l[4 * k : 4 * k + 4, :] = res_ref[:, k * CH : (k + 1) * CH].astype(F32)
        gain_l[4 * k : 4 * k + 4, :] = jnp.broadcast_to(gain_ref[k * CH : (k + 1) * CH].reshape(1, CH), (4, CH))

    hear(2)

    zeros64 = jnp.zeros((256, 64), F32)
    qr = qr_ref[...].astype(F32)
    q_l[...] = jnp.concatenate([qr, zeros64], axis=1).astype(BF16)
    q_r[...] = jnp.concatenate([zeros64, qr], axis=1).astype(BF16)
    newk[...] = jnp.zeros_like(newk)
    newr[...] = jnp.zeros_like(newr)
    for r in range(2):
        newk[2 * r : 2 * r + 2, :] = nl_ref[r].astype(F32)
        newr[2 * r : 2 * r + 2, 0:64] = nr_ref[r].astype(F32)
    nk = newk[...].astype(BF16)
    s = (dot_nt(q_ref[...], nk) + dot_nt(q_l[...], newr[...].astype(BF16))) * SCORE_SCALE
    row = iota((256, 128), 0)
    col = iota((256, 128), 1)
    ok = (col < 4) & (col // 2 == row // 128) & (col % 2 <= (row // 64) % 2)
    s = jnp.where(ok, s, NEG)
    m = jnp.max(s, -1, keepdims=True)
    p = jnp.exp(s - m)
    m_s[...] = jnp.broadcast_to(m, (256, 128))
    l_s[...] = jnp.broadcast_to(jnp.sum(p, -1, keepdims=True), (256, 128))
    o_s[...] = dot(p.astype(BF16), nk)

    def attend(keys, s_rope, scale, bias0, bias1):
        s = (dot_nt(q_ref[...], keys) + s_rope) * (scale * SCORE_SCALE)
        s = jnp.concatenate([s[:128] + bias0, s[128:] + bias1], axis=0)
        m_old = m_s[:, 0:1]
        m_new = jnp.maximum(m_old, jnp.max(s, -1, keepdims=True))
        p = jnp.exp(s - m_new)
        alpha = jnp.exp(m_old - m_new)
        m_s[...] = jnp.broadcast_to(m_new, (256, 128))
        l_s[...] = jnp.broadcast_to(l_s[:, 0:1] * alpha + jnp.sum(p, -1, keepdims=True), (256, 128))
        o_s[...] = o_s[...] * alpha + dot((p * scale).astype(BF16), keys)

    @pl.loop(0, 12)
    def _(n):
        keys = lat_v[pl.ds(n * 4, 4)].reshape(256, 512)
        ropes = rope_ref[pl.ds(n * 4, 4)].reshape(256, 128)
        sc = [scale_of(n * 4 + m) for m in range(4)]
        scale = jnp.concatenate([jnp.where(low1, sc[0], sc[1]), jnp.where(low1, sc[2], sc[3])], axis=1)
        attend(keys, dot_nt(q_l[...], ropes), scale, bias_of(0, n * 4), bias_of(1, n * 4))

    def attend_moved(k, lat_at, rope_at):
        source = ((x - k // 2 + 4) % 4) * 2 + (c + k % 2) % 2
        v = 48 + source * 4
        ropes = rope_at[0:128, :]
        lo = dot_nt(q_l[...], ropes)
        hi = dot_nt(q_r[...], ropes)
        s_rope = jnp.concatenate([lo[:, :64], hi[:, :64], lo[:, 64:], hi[:, 64:]], axis=1)
        sc = rope_at[128:144, :].astype(F32)
        scale = jnp.concatenate([sc[0:1], sc[1:2]], axis=1)
        attend(lat_at[...], s_rope, scale, bias_of(0, v), bias_of(1, v))

    attend_moved(0, slat.at[0], srope.at[0])

    def moved_from(k):
        page_copy(k, 0).wait_recv()
        page_copy(k, 1).wait_recv()
        attend_moved(k, rlat.at[k], rrope.at[k])

    def pass_on(kind):
        w_copy(kind, 0).wait_recv()
        if kind < 2:
            w_copy(kind, 2).start()
        w_copy(kind, 4).start()
        w_copy(kind, 1).wait_recv()
        if kind < 2:
            w_copy(kind, 3).start()
        w_copy(kind, 5).start()

    pass_on(0)
    pass_on(1)

    @pl.loop(4, 6)
    def _(k):
        moved_from(k)

    pass_on(2)

    moved_from(1)

    @pl.loop(0, 4)
    def _(n):
        moved_from(2 + (n % 2) * 4 + n // 2)

    o = (o_s[...] / l_s[:, 0:1]).astype(BF16)
    pr = iota((256, 256), 0)
    pc = iota((256, 256), 1)
    source = (pr // 8 % 4) * 64 + ((y + pr // 2 % 4) % 4) * 16 + (pr // 32) * 2 + pr % 2
    perm = jnp.where(pc == source, 1.0, 0.0).astype(BF16)
    so[...] = dot(perm, o).astype(BF16).reshape(8, 32, CH)

    def o_copy(n):
        return rcopy(so.at[(z + n) % 8], ro.at[n], o_ss.at[n], o_rs.at[n], (i, ex_at(0, n)))

    for n in (4, 3, 5, 2, 6, 1, 7):
        o_copy(n).start()
    ro[0] = so[z]
    for kind in range(2):
        w_copy(kind, 2).wait_recv()
        w_copy(kind, 3).wait_recv()
        w_copy(kind, 6).start()
    for n in range(1, 8):
        o_copy(n).wait_recv()

    for n in (4, 5, 6):
        w_copy(0, n).wait_recv()

    wcat = jnp.concatenate([wuv[d, h] for d in range(4) for h in range(2)], axis=1)
    hv = dot(ro[...].reshape(256, CH), wcat)
    hv = jnp.where(iota((256, 1024), 0) % 8 == iota((256, 1024), 1) // 128, hv, 0.0).astype(BF16)
    fr_, fc = iota((32, 256), 0), iota((32, 256), 1)
    fold = jnp.where(fc // 8 == ((z - fr_ // 4 + 8) % 8) * 4 + fr_ % 4, 1.0, 0.0).astype(BF16)
    hv = dot(fold, hv).astype(BF16)
    for kind, n in ((1, 4), (1, 5), (1, 6), (2, 4), (2, 5)):
        w_copy(kind, n).wait_recv()
    def z_copy(n, part):
        rows = pl.ds(part * 16, 16)
        return rcopy(
            sp2.at[(z + n) % 8, rows], pr2.at[n, rows], p2_s.at[part, n], p2_r.at[part, n], (i, ex_at(0, n))
        )

    far_first = (4, 3, 5, 2, 6, 1, 7)
    for part in range(2):
        for k in range(4 * part, min(4 * part + 4, NK)):
            w = slice(k * CH, (k + 1) * CH)
            s_f[:, w] = sum(dot(hv[:, d * 256 : (d + 1) * 256], wout[d, :, w]) for d in range(4))
            for zz in range(8):
                d_f[zz, 4 * k : 4 * k + 4, :] = s_f[4 * zz : 4 * zz + 4, w]
        sp2[:, 16 * part : 16 * part + 16, :] = d_f[:, 16 * part : 16 * part + 16, :].astype(BF16)
        for n in far_first:
            z_copy(n, part).start()
    total = d_f[z]
    for n in range(1, 8):
        z_copy(n, 0).wait_recv()
        z_copy(n, 1).wait_recv()
        total = total + pr2[n].astype(F32)
    al_f[...] = total

    hidden = (res_l[...] + total).astype(BF16).astype(F32)
    same = jnp.where(r32 % 4 == e32 % 4, 1.0, 0.0)
    sq = jnp.broadcast_to(jnp.sum(hidden * hidden, -1, keepdims=True), (32, 128))
    sq = jnp.dot(same, sq, precision=lax.Precision.HIGHEST, preferred_element_type=F32)
    normed = (hidden * lax.rsqrt(sq[:, 0:1] / D + NORM_EPS) * gain_l[...]).astype(BF16)
    sd[...] = dot(q_s[...], normed).astype(BF16).reshape(32, 16, CH)

    def d_copy(k):
        e = ex_at(k // 8, k % 8)
        return rcopy(sd.at[e], rd.at[k], d_ss.at[k], d_rs.at[k], (i, e))

    for dy in range(4):
        for dz in (4, 3, 5, 2, 6, 1, 7, 0):
            if dy or dz:
                d_copy(dy * 8 + dz).start()

    rd[0] = sd[j]

    acc = jnp.zeros((32, 32), F32)
    for k in range(NK):
        lg = dot_nt(normed, wr_ref[:, k * CH : (k + 1) * CH])
        acc = acc + jnp.where(r32 // 4 == k, lg, 0.0)
    logits = jnp.dot(same, acc, precision=lax.Precision.HIGHEST, preferred_element_type=F32)
    sig = sel / (1.0 + jnp.exp(-logits))
    gates = ROUTE_SCALE * sig / jnp.sum(sig, -1, keepdims=True)
    g_hi = gates.astype(BF16)
    g_lo = (gates - g_hi.astype(F32)).astype(BF16)
    c_s[0] = (dot(g_hi, spread) * qt_s[...]).astype(BF16)
    c_s[1] = (dot(g_lo, spread) * qt_s[...]).astype(BF16)
    for k in range(NK):
        out_ref[0:4, k * CH : (k + 1) * CH] = al_f[4 * k : 4 * k + 4, :].astype(BF16)
    for n in range(16, 19):
        loads[n].wait()

    def ag(g, n):
        lo, hi = pl.ds(0, HALF), pl.ds(HALF, HALF)
        src, dst, dev = [
            (xr.at[g, 0, :, lo], xr.at[g, 3, :, lo], right),
            (xr.at[g, 0, :, hi], xr.at[g, 1, :, hi], left),
            (xr.at[g, 3, :, lo], xr.at[g, 2, :, lo], right),
            (xr.at[g, 1, :, hi], xr.at[g, 2, :, hi], left),
            (xr.at[g, 0], xr.at[g, 4], sib),
            (xr.at[g, 3], xr.at[g, 7], sib),
            (xr.at[g, 1], xr.at[g, 5], sib),
            (xr.at[g, 2], xr.at[g, 6], sib),
            (xr.at[g, 0, :, hi], xr.at[g, 3, :, hi], right),
            (xr.at[g, 0, :, lo], xr.at[g, 1, :, lo], left),
        ][n]
        return rcopy(src, dst, ag_s.at[g, n], ag_r.at[g, n], dev)

    def rs(g, n):
        lo, hi = pl.ds(0, HALF), pl.ds(HALF, HALF)
        src, dst, dev = [
            (pp.at[g, pl.ds(4, 4)], sr.at[g], sib),
            (hb.at[g, :, lo], hr.at[g, 0], right),
            (hb.at[g, :, hi], hr.at[g, 1], left),
            (fb.at[g, 0, :, hi], fr.at[g, 0, :, hi], right),
            (fb.at[g, 1, :, lo], fr.at[g, 1, :, lo], left),
            (fb.at[g, 0, :, lo], fr.at[g, 0, :, lo], right),
            (fb.at[g, 1, :, hi], fr.at[g, 1, :, hi], left),
        ][n]
        return rcopy(src, dst, rs_s.at[g, n], rs_r.at[g, n], dev)

    def b_copy(k):
        e = ex_at(-(k // 8), -(k % 8))
        return rcopy(sret.at[k], rret.at[j], b_ss.at[k], b_rs.at[k], (i, e))

    def stage_a(g):
        @pl.loop(0, 8)
        def _(n):
            @pl.when(g * 8 + n > 0)
            def _():
                d_copy(g * 8 + n).wait_recv()

        got = rd[pl.ds(g * 8, 8)].reshape(128, CH).astype(F32)
        for b in range(4):
            t_f[b * 128 : (b + 1) * 128, :] = got[:, b * 128 : (b + 1) * 128]
        for k in range(NK):
            for b in range(4):
                at = k * CH + b * 128
                xr[g, 0, :, at : at + 128] = t_f[pl.ds(b * 128 + k, 16, stride=8), :].astype(BF16)
        for n in (0, 1, 8, 9, 4):
            ag(g, n).start()

    def stage_b(g):
        ag(g, 0).wait_recv()
        ag(g, 2).start()
        ag(g, 1).wait_recv()
        ag(g, 3).start()
        ag(g, 8).wait_recv()
        ag(g, 5).start()
        ag(g, 9).wait_recv()
        ag(g, 6).start()

    def stage_c(g):
        ag(g, 2).wait_recv()
        ag(g, 3).wait_recv()
        ag(g, 7).start()
        for n in range(4, 8):
            ag(g, n).wait_recv()

    def stage_d(g):
        rows = xr[g].reshape(128, D)
        gate = dot(rows, wg[...])
        up = dot(rows, wu[...])
        h = (gate / (1.0 + jnp.exp(-gate)) * up).astype(BF16)
        for k in range(NK):
            w = slice(k * CH, (k + 1) * CH)
            pp[g, :, :, w] = dot(h, wd[:, w]).astype(BF16).reshape(8, 16, CH)
        rs(g, 0).start()

    def stage_e(g):
        rs(g, 0).wait_recv()
        hb[g] = (pp[g, 2].astype(F32) + sr[g, 2].astype(F32)).astype(BF16)
        rs(g, 1).start()
        rs(g, 2).start()
        ss[g] = pp[g, 0:4].astype(F32) + sr[g].astype(F32)
        fb[g, 0, :, HALF:] = ss[g, 1, :, HALF:].astype(BF16)
        fb[g, 1, :, 0:HALF] = ss[g, 3, :, 0:HALF].astype(BF16)
        rs(g, 3).start()
        rs(g, 4).start()

    def stage_f(g):
        rs(g, 1).wait_recv()
        fb[g, 0, :, 0:HALF] = (ss[g, 1, :, 0:HALF] + hr[g, 0].astype(F32)).astype(BF16)
        rs(g, 5).start()
        rs(g, 2).wait_recv()
        fb[g, 1, :, HALF:] = (ss[g, 3, :, HALF:] + hr[g, 1].astype(F32)).astype(BF16)
        rs(g, 6).start()

    def stage_g(g):
        for n in range(3, 7):
            rs(g, n).wait_recv()
        for b in range(4):
            for k in range(NK):
                w = slice(k * CH + b * 128, k * CH + b * 128 + 128)
                v = ss[g, 0, :, w] + fr[g, 0, :, w].astype(F32) + fr[g, 1, :, w].astype(F32)
                t_f[pl.ds(b * 128 + k, 16, stride=8), :] = v
            t_f[pl.ds(b * 128 + 7, 16, stride=8), :] = jnp.zeros((16, 128), F32)
        back = jnp.concatenate([t_f[b * 128 : (b + 1) * 128, :] for b in range(4)], axis=1)
        sret[pl.ds(g * 8, 8)] = back.astype(BF16).reshape(8, 16, CH)

        for n in (4, 3, 5, 2, 6, 1, 7):
            b_copy(g * 8 + n).start()

        @pl.when(g > 0)
        def _():
            b_copy(g * 8).start()

    stages = [(stage_a, 0), (stage_b, 1), (stage_c, 2), (stage_d, 2), (stage_e, 3), (stage_f, 4), (stage_g, 5)]

    @pl.loop(0, 9)
    def _(t):
        for fn, lag in stages:

            @pl.when((t >= lag) & (t < lag + 4))
            def _(fn=fn, lag=lag):
                fn(t - lag)

    rret[j] = sret[0]

    @pl.loop(1, 8)
    def _(k):
        page_copy(k, 0).wait_send()
        page_copy(k, 1).wait_send()

    for kind in range(3):
        for n in range(7):
            if kind < 2 or n in (0, 1, 4, 5):
                w_copy(kind, n).wait_send()
    for n in range(1, 8):
        o_copy(n).wait_send()
        z_copy(n, 0).wait_send()
        z_copy(n, 1).wait_send()

    @pl.loop(0, 4)
    def _(g):
        for n in range(10):
            ag(g, n).wait_send()
        for n in range(7):
            rs(g, n).wait_send()

    @pl.loop(1, 32)
    def _(k):
        d_copy(k).wait_send()
        b_copy(k).wait_send()

    al_f[...] = jnp.zeros_like(al_f)
    for g in range(4):
        for n in range(8):
            if g * 8 + n:
                b_copy(g * 8 + n).wait_recv()
        group = (y + g) % 4
        rows = rret[pl.ds(group * 8, 8)].reshape(128, CH)
        lanes = pl.ds(pl.multiple_of(group * 128, 128), 128)
        al_f[...] += dot(c_s[0, :, lanes], rows) + dot(c_s[1, :, lanes], rows)
    for k in range(NK):
        out_ref[4:8, k * CH : (k + 1) * CH] = al_f[4 * k : 4 * k + 4, :].astype(BF16)


def body(
    cache_lat, cache_rope, page_scale, move_list, page_table, lengths, q_lat, q_rope, new_lat, new_rope,
    w_uv, w_out, residual, norm_gain, w_router, routes, w_gate, w_up, w_down,
):
    any_spec = pl.BlockSpec(memory_space=pl.ANY)
    vmem = pl.BlockSpec(memory_space=pltpu.VMEM)
    dma = pltpu.SemaphoreType.DMA
    vm = pltpu.VMEM
    operands = (
        move_list.transpose(0, 2, 1), page_scale, lengths, page_table, cache_lat, cache_rope,
        q_lat.reshape(256, 512), q_rope.reshape(256, 64), new_lat, new_rope, w_uv, w_out, residual,
        norm_gain, w_router.T, routes, w_gate, w_up, w_down,
    )
    out = pl.pallas_call(
        kernel,
        out_shape=pltpu.VMEM((8, D), BF16),
        in_specs=[any_spec] * len(operands),
        out_specs=vmem,
        scratch_shapes=[
            pltpu.SMEM((4, 8), jnp.int32), vm((48,), BF16), pltpu.SMEM((2,), jnp.int32), vm((2, 32), jnp.int32),
            vm((48, 4096), BF16), vm((256, 512), BF16), vm((256, 64), BF16), vm((2, 2, 512), BF16), vm((2, 2, 64), BF16),
            vm((4, D), BF16), vm((D,), F32), vm((32, D), BF16), vm((4, 8), jnp.int32),
            vm((48 * 64, 128), F32), vm((48, 64, 128), BF16), vm((2, 80, 128), F32), vm((128, 128), F32), vm((32, 8), jnp.int32),
            vm((48, 64, 512), BF16), vm((4, 2, 512, 128), BF16), vm((4, 256, D), BF16),
            vm((D, 256), BF16), vm((D, 256), BF16), vm((256, D), BF16),
            vm((8, 256, 512), BF16), vm((8, 144, 128), BF16), vm((8, 256, 512), BF16), vm((8, 144, 128), BF16),
            vm((128, 512), F32), vm((128, 128), F32), vm((256, 128), BF16), vm((256, 128), BF16),
            vm((256, 128), F32), vm((256, 128), F32), vm((256, 512), F32),
            vm((8, 32, CH), BF16), vm((8, 32, CH), BF16), vm((32, D), F32),
            vm((8, 32, CH), F32), vm((8, 32, CH), BF16), vm((8, 32, CH), BF16),
            vm((32, CH), F32), vm((32, CH), F32), vm((32, CH), F32),
            vm((512, 32), BF16), vm((32, 512), F32), vm((2, 32, 512), BF16), vm((32, 16, CH), BF16), vm((32, 16, CH), BF16),
            vm((512, 128), F32), vm((4, 8, 16, D), BF16), vm((4, 8, 16, D), BF16), vm((4, 4, 16, D), BF16),
            vm((4, 4, 16, D), F32), vm((4, 16, D), BF16), vm((4, 2, 16, HALF), BF16),
            vm((4, 2, 16, D), BF16), vm((4, 2, 16, D), BF16), vm((32, 16, CH), BF16), vm((32, 16, CH), BF16),
            dma((19,)), dma((2, 8)), dma((2, 8)), dma((3, 7)), dma((3, 7)), dma((8,)), dma((8,)),
            dma((2, 8)), dma((2, 8)), dma((32,)), dma((32,)), dma((4, 10)), dma((4, 10)), dma((4, 7)), dma((4, 7)),
            dma((32,)), dma((32,)), pltpu.SemaphoreType.REGULAR((3,)),
        ],
        compiler_params=pltpu.CompilerParams(
            collective_id=0, has_side_effects=True, vmem_limit_bytes=60 * 2**20
        ),
        name="step",
    )(*operands)
    return out[:4], out[4:]


def solution(mesh):
    both = ("dp", "expert")
    return jax.shard_map(
        body,
        mesh=mesh,
        in_specs=(
            P(both, None, None), P(both, None), P(both), P(both, None, None), P(both, None), P(both),
            P(both, None, None, None), P(both, None, None, None), P(both, None, None), P(both, None, None),
            P("expert", None, None), P("expert", None), P(both, None), P(), P(), P(both, None),
            P("expert", None, "dp"), P("expert", None, "dp"), P("expert", "dp", None),
        ),
        out_specs=(P(both, None), P(both, None)),
        check_vma=False,
    )
```
